256 devices in a mesh: section: 4 (over y), grp: 4 (over x), tp: 16 (over z, core).
Axes of the slice: x: 4, y: 4, z: 8, core: 2. Of those that a mesh axis runs over, the one named last changes fastest.
Arguments:
- ctx_latent: bfloat16 [48, 1024, 512], P(('section', 'grp'), 'tp'), may hold values from -4 to 4
- ctx_rope: bfloat16 [48, 512, 128], P(('section', 'grp'), 'tp'), may hold values from -4 to 4
- ctx_scale: bfloat16 [48, 1024, 4], P(('section', 'grp'), 'tp'), may hold values from 0.5 to 2
- dest: int32 [48], replicated, may hold values from 0 to 3, as said below
- ctx_len: int32 [48], P(('section', 'grp')), may hold values from 256 to 1024
- queries: bfloat16 [48, 32, 36864], P(('section', 'grp'), None, 'tp'), may hold values from -100 to 100
- reply_keys: bfloat16 [48, 8, 2304], P(('section', 'grp')), may hold values from -4 to 4
- reply_len: int32 [48, 8], P(('section', 'grp')), may hold values from 1 to 4
- targets: int32 [48, 32], P(('section', 'grp')), may hold values from 0 to 4095
- w_uv: bfloat16 [512, 8192], P(None, 'tp'), may hold values from -0.25 to 0.25
- w_out: bfloat16 [8192, 7168], P('tp'), may hold values from -0.0625 to 0.0625
- w_vocab: bfloat16 [7168, 4096], P(None, 'tp')
Outputs:
- scores: float32 [48, 8], P(('section', 'grp'))
The draws below stay inside these ranges and needn't reach their ends.
Inputs may be any that keep to these rules, and one draw needn't show every extreme that they name: `dest`: within each row of section, every decode group receives exactly 3 requests; one prefill group sends at most 2 requests to one decode group, and some prefill group sends 2 to one decode group in every draw.
All inputs are finite; a program needn't handle non-finite values.
Results may differ from the reference program's by a relative error of at most 0.0037.
Values may be sent and summed in bfloat16 or wider, within the bound.
A program may use at most 128 MiB of HBM per device.

```python
import math
import jax
import jax.numpy as jnp
import numpy as np
from jax import lax

D = 7168
H = 64
KVR = 512
ROPE = 64
VHD = 128
BLK = 128
CTX = 1024
CAND = 8
STEPS = 4
R_SRC = 3
REQS = 48
VOCAB = 4096
N_SECTION = 4
N_GRP = 4


def draw_dest(key, part):
    key = jax.random.fold_in(key, 11)
    starting = jax.random.randint(jax.random.fold_in(key, 1), (N_SECTION,), 0, N_GRP)
    another = (starting + jax.random.randint(jax.random.fold_in(key, 2), (N_SECTION,), 1, N_GRP)) % N_GRP
    section_keys = jax.random.split(jax.random.fold_in(key, 3), N_SECTION)
    labels = jax.vmap(lambda one_key: jax.random.permutation(one_key, N_GRP))(section_keys)
    offsets = jnp.stack([starting, starting, another], axis=1)
    group_keys = jax.random.split(jax.random.fold_in(key, 4), N_SECTION * N_GRP)
    orders = jax.vmap(lambda one_key: jax.random.permutation(one_key, R_SRC))(group_keys).reshape(N_SECTION, N_GRP, R_SRC)
    spread = jnp.broadcast_to(offsets[:, None, :], (N_SECTION, N_GRP, R_SRC))
    shuffled = jnp.take_along_axis(spread, orders, axis=2)
    shifted = (jnp.arange(N_GRP, dtype=jnp.int32)[None, :, None] + shuffled) % N_GRP
    chosen = jnp.take_along_axis(labels, shifted.reshape(N_SECTION, N_GRP * R_SRC), axis=1)
    return chosen.reshape(N_SECTION * N_GRP * R_SRC).astype(jnp.int32)


def draw_ctx_len(key, part):
    key = jax.random.fold_in(key, 12)
    lengths = jax.random.randint(jax.random.fold_in(key, 1), (REQS,), CTX // 4, CTX + 1)
    picked = jax.random.permutation(jax.random.fold_in(key, 2), REQS)
    lengths = lengths.at[picked[0]].set(CTX).at[picked[1]].set(CTX // 4)
    return lengths.astype(jnp.int32)


def draw_queries(key, part):
    key = jax.random.fold_in(key, 13)
    values = jax.random.normal(jax.random.fold_in(key, 1), (REQS, CAND * STEPS, H * (KVR + ROPE)), jnp.float32)
    values = jnp.clip(values, -4.0, 4.0)
    return values.astype(jnp.bfloat16)


def draw_w_vocab(key, part):
    key = jax.random.fold_in(key, 14)
    values = jnp.clip(jax.random.normal(jax.random.fold_in(key, 1), (D, VOCAB), jnp.float32), -4.0, 4.0)
    values = values * (3.0 / math.sqrt(D))
    return values.astype(jnp.bfloat16)


def with_ends(values, rng, low, high):
    index_at = [jax.random.randint(jax.random.fold_in(rng, axis), (), 0, length) for axis, length in enumerate(values.shape)]
    main_axis = values.shape.index(max(values.shape))
    next_to = index_at[:main_axis] + [(index_at[main_axis] + 1) % values.shape[main_axis]] + index_at[main_axis + 1:]
    return values.at[tuple(index_at)].set(low).at[tuple(next_to)].set(high)


def block_levels(key, extent, cuts, smallest, largest):
    loudness, own = 1.0, jax.random.fold_in(key, 6)
    for position, blocks in cuts:
        heights = jnp.exp(jax.random.uniform(jax.random.fold_in(own, position), (blocks,), jnp.float32, smallest / len(cuts), largest / len(cuts)))
        loudness = loudness * jnp.repeat(heights, extent[position] // blocks).reshape([-1 if axis == position else 1 for axis in range(len(extent))])
    return loudness


def rank_table(count, lean):
    portions = [(1 << 20) // math.isqrt(standing ** lean) + 1 for standing in range(1, count + 1)]
    scale = 1 + sum(portions) // (1 << 30)
    return np.cumsum(np.array([max(1, weight // scale) for weight in portions]))


def skewed_ids(key, extent, count, lean):
    table = rank_table(count, lean)
    lot = jax.random.randint(jax.random.fold_in(key, 1), extent, 0, int(table[count - 1]))
    rank = jnp.searchsorted(jnp.asarray(table, jnp.int32), lot, side="right")
    return jax.random.permutation(jax.random.fold_in(key, 2), count)[rank].astype(jnp.int32)


def normal_values(key, dims, scale, bound, cuts=(), kind=jnp.bfloat16):
    level = block_levels(key, dims, cuts, -0.22, 0.18) if cuts else 1.0
    entries = jax.random.normal(key, dims, jnp.float32) * scale * level
    return jnp.minimum(jnp.maximum(entries, -bound), bound).astype(kind)


def setup_inputs(seed: int = 0) -> dict:
    key_list = jax.random.split(jax.random.key(seed), 13)
    ctx_latent = normal_values(key_list[0], (REQS, CTX, KVR), 1.0, 4.0, ((0, 16), (1, 16)))
    ctx_rope = normal_values(key_list[1], (REQS, CTX // 2, 2 * ROPE), 1.0, 4.0, ((0, 16), (1, 16)))
    ctx_scale = jnp.clip(jnp.exp(math.log(2.0) - 1.3862944 * jax.random.uniform(key_list[2], (REQS, CTX, KVR // BLK), jnp.float32) ** block_levels(key_list[2], (REQS, CTX, KVR // BLK), ((0, 16), (1, 16)), -0.2, 0.2)), 0.5, 2.0).astype(jnp.bfloat16)
    dest = draw_dest(jax.random.fold_in(key_list[12], 71), 0)
    ctx_len = draw_ctx_len(jax.random.fold_in(key_list[12], 71), 0)
    queries = draw_queries(jax.random.fold_in(key_list[12], 71), 0)
    reply_keys = normal_values(key_list[6], (REQS, CAND, STEPS * (KVR + ROPE)), 1.0, 4.0, ((0, 16),))
    reply_len = with_ends(jax.random.randint(key_list[7], (REQS, CAND), 1, STEPS + 1), jax.random.fold_in(key_list[7], 1), 1, STEPS).astype(jnp.int32)
    targets = with_ends(skewed_ids(key_list[8], (REQS, CAND * STEPS), VOCAB, 2), jax.random.fold_in(key_list[8], 3), 0, VOCAB - 1).astype(jnp.int32)
    w_uv = normal_values(key_list[9], (KVR, H * VHD), KVR ** -0.5, 0.25, ((1, 16),))
    w_out = normal_values(key_list[10], (H * VHD, D), (H * VHD) ** -0.5, 0.0625, ((0, 16),))
    w_vocab = draw_w_vocab(jax.random.fold_in(key_list[12], 71), 0)
    return dict(ctx_latent=ctx_latent, ctx_rope=ctx_rope, ctx_scale=ctx_scale, dest=dest, ctx_len=ctx_len, queries=queries, reply_keys=reply_keys, reply_len=reply_len, targets=targets, w_uv=w_uv, w_out=w_out, w_vocab=w_vocab)


softmax_scale = 192.0 ** (-0.5)
norm_epsilon = 1e-06

def receive_order(dest):
    per_section = N_GRP * R_SRC
    grid = dest.reshape(N_SECTION, per_section)
    sort_keys = grid * per_section + jnp.arange(per_section, dtype=jnp.int32)[None, :]
    ordered = jnp.argsort(sort_keys, axis=1).astype(jnp.int32)
    anchors = ordered + (jnp.arange(N_SECTION, dtype=jnp.int32) * per_section)[:, None]
    return jnp.roll(anchors, 1, axis=0).reshape(N_SECTION * per_section)

def rounded(values):
    return lax.optimization_barrier(values.astype(jnp.bfloat16)).astype(jnp.float32)

def reference(ctx_latent, ctx_rope, ctx_scale, dest, ctx_len, queries, reply_keys, reply_len, targets, w_uv, w_out, w_vocab):
    source = receive_order(dest)
    w_heads = w_uv.astype(jnp.float32).reshape(KVR, H, VHD)

    def one_request(inputs):
        anchor, context_length, query_rows, reply_rows, lengths, target_rows = inputs
        latent = ctx_latent[anchor].astype(jnp.float32).reshape(CTX, KVR // BLK, BLK)
        scaled = latent * ctx_scale[anchor].astype(jnp.float32)[:, :, None]
        dequant = rounded(scaled.reshape(CTX, KVR))
        rope_keys = ctx_rope[anchor].astype(jnp.float32).reshape(CTX, ROPE)
        query = query_rows.astype(jnp.float32).reshape(CAND, STEPS, H, KVR + ROPE)
        reply = reply_rows.astype(jnp.float32).reshape(CAND, STEPS, KVR + ROPE)
        context_scores = jnp.einsum('athk,pk->athp', query[..., :KVR], dequant)
        context_scores = (context_scores + jnp.einsum('athk,pk->athp', query[..., KVR:], rope_keys)) * softmax_scale
        visible = jnp.arange(CTX, dtype=jnp.int32) < context_length
        context_scores = jnp.where(visible[None, None, None, :], context_scores, -jnp.inf)
        reply_scores = jnp.einsum('athk,auk->athu', query, reply) * softmax_scale
        causal = jnp.arange(STEPS, dtype=jnp.int32)[None, :] <= jnp.arange(STEPS, dtype=jnp.int32)[:, None]
        reply_scores = jnp.where(causal[None, :, None, :], reply_scores, -jnp.inf)
        row_top = jnp.maximum(lax.optimization_barrier(jnp.max(context_scores, axis=3)), lax.optimization_barrier(jnp.max(reply_scores, axis=3)))[..., None]
        context_exp = jnp.exp(context_scores - row_top)
        reply_exp = jnp.exp(reply_scores - row_top)
        row_total = lax.optimization_barrier(jnp.sum(context_exp, axis=3, keepdims=True)) + lax.optimization_barrier(jnp.sum(reply_exp, axis=3, keepdims=True))
        context_weight = rounded(context_exp / row_total)
        reply_weight = rounded(reply_exp / row_total)
        attended = jnp.einsum('athp,pk->athk', context_weight, dequant)
        attended = rounded(attended + jnp.einsum('athu,auk->athk', reply_weight, reply[..., :KVR]))
        head_value = jnp.einsum('athk,khv->athv', attended, w_heads).astype(jnp.bfloat16)
        hidden = jnp.dot(head_value.reshape(CAND * STEPS, H * VHD), w_out, preferred_element_type=jnp.float32)
        normed = (hidden * lax.rsqrt(lax.optimization_barrier(jnp.mean(hidden * hidden, axis=1, keepdims=True)) + norm_epsilon)).astype(jnp.bfloat16)
        logits = jnp.dot(normed, w_vocab, preferred_element_type=jnp.float32)
        log_total = jax.nn.logsumexp(logits, axis=1)
        target_logit = jnp.take_along_axis(logits, target_rows[:, None], axis=1)[:, 0]
        log_prob = (target_logit - log_total).reshape(CAND, STEPS)
        inside = jnp.arange(STEPS, dtype=jnp.int32)[None, :] < lengths[:, None]
        return lax.optimization_barrier(jnp.sum(jnp.where(inside, log_prob, 0.0), axis=1)) / lengths.astype(jnp.float32)
    return lax.map(one_request, (source, ctx_len, queries, reply_keys, reply_len, targets))
```

```python
import functools

import jax
import jax.numpy as jnp
from jax import lax
from jax.experimental import pallas as pl
from jax.experimental.pallas import tpu as pltpu
from jax.sharding import PartitionSpec as P

MESH = pl.DeviceIdType.MESH
BF16, F32 = jnp.bfloat16, jnp.float32

softmax_scale = 192.0 ** (-0.5)
norm_epsilon = 1e-06

NS, NG, NZ, NT = 4, 4, 8, 16
REQ, CAND, STEPS, HEADS = 3, 8, 4, 4
KVR, ROPE, KEY = 512, 64, 576
ROWS = REQ * CAND * STEPS
QROWS = HEADS * CAND * STEPS
D, HALF = 7168, 3584
BR, BC = 48, 896
HOP_A, HOP_B = 4, 3
PACK = 1152
VOCAB_LOCAL = 256


def nt_dot(a, b):
    return lax.dot_general(a, b, (((1,), (1,)), ((), ())), preferred_element_type=F32)


def nn_dot(a, b):
    return lax.dot_general(a, b, (((1,), (0,)), ((), ())), preferred_element_type=F32)


def unpack_key(slab, index):
    n = slab.shape[0]
    low = lax.broadcasted_iota(jnp.int32, (n, 128), 1) < ROPE
    start = index * KEY
    first = start // 128
    if index % 2 == 0:
        latent = slab[:, start : start + KVR]
        tile = slab[:, start + KVR : start + KVR + 128]
        rope_low = jnp.where(low, tile, 0.0)
        rope_high = pltpu.roll(rope_low, 64, 1)
    else:
        turned = [
            pltpu.roll(slab[:, (first + j) * 128 : (first + j + 1) * 128], 64, 1) for j in range(5)
        ]
        latent = jnp.concatenate([jnp.where(low, turned[j], turned[j + 1]) for j in range(4)], axis=1)
        rope_low = jnp.where(low, turned[4], 0.0)
        rope_high = pltpu.roll(rope_low, 64, 1)
    return latent, rope_low, rope_high


def kernel(
    dest, ctx_len, reply_len, lat_ref, rope_ref, scale_ref, reply_ref, target_ref,
    query_hbm, uv_hbm, out_hbm, vocab_hbm,
    score_ref,
    xsrc, sbuf, rbuf_0, rbuf_1, ctx, q_in, qn, qr, rkn, rkr, m_s, l_s, acc_s, att, hvbuf, wuv, wout, wvoc,
    snd_a, snd_b, rcv_a, rcv_b, hid, lg, ss, stat,
    local_sem, route_send, route_recv, ctx_send, ctx_recv, w_send, w_recv, hv_send, hv_recv,
    ra_send, ra_recv, rb_send, rb_recv, h_send, h_recv, st_send, st_recv,
):
    s, g, t = lax.axis_index("section"), lax.axis_index("grp"), lax.axis_index("tp")
    z, c = t // 2, t % 2
    sib = t + 1 - 2 * c
    sgn = 1 - 2 * c
    rbuf = (rbuf_0, rbuf_1)
    next_s = lax.rem(s + 1, NS)
    prev_s = lax.rem(s + NS - 1, NS)

    def ring(step):
        return lax.rem(z + sgn * step + 2 * NZ, NZ)

    dev_a = {"tp": ring(1) * 2 + c}
    dev_b = {"tp": ring(-1) * 2 + c}
    dev_sib = {"tp": sib}

    barrier = pltpu.get_barrier_semaphore()
    for k in range(NG):
        pl.semaphore_signal(barrier, inc=1, device_id={"section": next_s, "grp": k}, device_id_type=MESH)
        pl.semaphore_signal(barrier, inc=1, device_id={"section": prev_s, "grp": k}, device_id_type=MESH)
    for d in range(1, NT):
        pl.semaphore_signal(barrier, inc=1, device_id={"tp": lax.rem(t + d, NT)}, device_id_type=MESH)

    own_cols = pl.ds(pl.multiple_of(c * HALF, 128), HALF)
    other_cols = pl.ds(pl.multiple_of((1 - c) * HALF, 128), HALF)
    local = [
        pltpu.make_async_copy(query_hbm, q_in, local_sem.at[0]),
        pltpu.make_async_copy(uv_hbm, wuv, local_sem.at[1]),
        pltpu.make_async_copy(out_hbm.at[:, own_cols], wout.at[c], local_sem.at[2]),
        pltpu.make_async_copy(vocab_hbm, wvoc, local_sem.at[3]),
    ]
    local[0].start()

    row = lax.broadcasted_iota(jnp.int32, (64, 64), 0)
    col = lax.broadcasted_iota(jnp.int32, (64, 64), 1)
    place = 2 * ((row // 32) * 16 + row % 16) + (row // 16) % 2
    perm = (col == place).astype(BF16)
    for j in range(REQ):
        scale = scale_ref[j].astype(F32)
        parts = [
            (lat_ref[j, :, b * 128 : (b + 1) * 128].astype(F32) * scale[:, b : b + 1]).astype(BF16)
            for b in range(4)
        ]
        moved = nn_dot(perm, jnp.concatenate(parts, axis=1)).astype(BF16)
        for h in range(2):
            xsrc[j, h, :, 0:KVR] = moved[h * 32 : h * 32 + 16]
            xsrc[j, h, :, KVR : 2 * KVR] = moved[h * 32 + 16 : h * 32 + 32]
            xsrc[j, h, :, 2 * KVR : PACK] = rope_ref[j, h * 16 : (h + 1) * 16, :]

    own_dest = [dest[(s * NG + g) * REQ + j] for j in range(REQ)]
    for h in range(2):
        for k in range(NG):
            first = jnp.where(own_dest[0] == k, 0, jnp.where(own_dest[1] == k, 1, 2))
            last = jnp.where(own_dest[2] == k, 2, jnp.where(own_dest[1] == k, 1, 0))
            sbuf[h, k, 0] = xsrc[first, h]
            sbuf[h, k, 1] = xsrc[last, h]

    pl.semaphore_wait(barrier, 2 * NG + NT - 1)

    def route(h, k):
        return pltpu.make_async_remote_copy(
            src_ref=sbuf.at[h, k], dst_ref=rbuf[h].at[pl.ds(2 * g, 2)],
            send_sem=route_send.at[h, k], recv_sem=route_recv.at[h, g],
            device_id={"section": next_s, "grp": k}, device_id_type=MESH,
        )

    def route_arrived(h, k):
        return pltpu.make_async_remote_copy(
            src_ref=sbuf.at[h, k], dst_ref=rbuf[h].at[pl.ds(2 * k, 2)],
            send_sem=route_send.at[h, k], recv_sem=route_recv.at[h, k],
            device_id={"section": next_s, "grp": k}, device_id_type=MESH,
        )

    for h in range(2):
        for k in range(NG):
            route(h, k).start()
    w_copy = pltpu.make_async_remote_copy(
        src_ref=out_hbm.at[:, other_cols], dst_ref=wout.at[c],
        send_sem=w_send, recv_sem=w_recv, device_id=dev_sib, device_id_type=MESH,
    )
    w_arrive = pltpu.make_async_remote_copy(
        src_ref=out_hbm.at[:, other_cols], dst_ref=wout.at[1 - c],
        send_sem=w_send, recv_sem=w_recv, device_id=dev_sib, device_id_type=MESH,
    )
    w_copy.start()
    for copy in local[1:]:
        copy.start()

    picks = [jnp.int32(0)] * REQ
    count = jnp.int32(0)
    for h in range(NG):
        seen = jnp.int32(0)
        for j in range(REQ):
            hit = dest[(prev_s * NG + h) * REQ + j] == g
            for k in range(REQ):
                picks[k] = jnp.where(jnp.logical_and(hit, count == k), h * 2 + seen, picks[k])
            one = jnp.where(hit, 1, 0)
            seen = seen + one
            count = count + one
    picks = [jnp.minimum(pick, 2 * NG - 1) for pick in picks]

    local[0].wait()
    a_row = (lax.broadcasted_iota(jnp.int32, (QROWS, 32), 0) % 32) // STEPS
    t_row = lax.broadcasted_iota(jnp.int32, (QROWS, 32), 0) % STEPS
    a_col = lax.broadcasted_iota(jnp.int32, (QROWS, 32), 1) % CAND
    u_col = lax.broadcasted_iota(jnp.int32, (QROWS, 32), 1) // CAND
    reply_seen = jnp.logical_and(a_row == a_col, u_col <= t_row)

    def prepare(k, carry):
        slab = q_in[k].astype(F32)
        for h in range(HEADS):
            latent, low, high = unpack_key(slab, h)
            qn[k, h * 32 : (h + 1) * 32, :] = latent.astype(BF16)
            qr[k, h * 32 : (h + 1) * 32, :] = low.astype(BF16)
            qr[k, QROWS + h * 32 : QROWS + (h + 1) * 32, :] = high.astype(BF16)
        keys = reply_ref[k].astype(F32)
        pieces = [unpack_key(keys, u) for u in range(STEPS)]
        rkn[...] = jnp.concatenate([piece[0] for piece in pieces], axis=0).astype(BF16)
        rkr[...] = jnp.concatenate([piece[1] for piece in pieces], axis=0).astype(BF16)
        scores = nt_dot(qn[k], rkn[...]) + nt_dot(qr[k, 0:QROWS], rkr[...])
        scores = jnp.where(reply_seen, scores * softmax_scale, -jnp.inf)
        top = jnp.max(scores, axis=1, keepdims=True)
        weight = jnp.exp(scores - top)
        m_s[k] = top
        l_s[k] = jnp.sum(weight, axis=1, keepdims=True)
        acc_s[k] = nn_dot(weight.astype(BF16), rkn[...])
        return carry

    lax.fori_loop(0, REQ, prepare, 0)

    def ctx_copy(h, k, slot, way, device):
        return pltpu.make_async_remote_copy(
            src_ref=ctx.at[h, k, slot], dst_ref=ctx.at[h, k, slot],
            send_sem=ctx_send.at[h, k, slot, way], recv_sem=ctx_recv.at[h, k, slot],
            device_id=device, device_id_type=MESH,
        )

    def open_half(h):
        for k in range(NG):
            route_arrived(h, k).wait_recv()
        for k in range(REQ):
            ctx[h, k, t] = rbuf[h][picks[k]]
            ctx_copy(h, k, t, 0, dev_a).start()
            ctx_copy(h, k, t, 1, dev_b).start()
            ctx_copy(h, k, t, 2, dev_sib).start()

    def hop(h, i):
        def one(k, carry):
            slot = ring(-i) * 2 + c
            ctx_copy(h, k, slot, 0, dev_a).wait_recv()

            @pl.when(i < HOP_A)
            def _():
                ctx_copy(h, k, slot, 0, dev_a).start()

            ctx_copy(h, k, slot, 2, dev_sib).start()

            @pl.when(i <= HOP_B)
            def _():
                slot_b = ring(i) * 2 + c
                ctx_copy(h, k, slot_b, 1, dev_b).wait_recv()

                @pl.when(i < HOP_B)
                def _():
                    ctx_copy(h, k, slot_b, 1, dev_b).start()

                ctx_copy(h, k, slot_b, 2, dev_sib).start()

            return carry

        lax.fori_loop(0, REQ, one, 0)

    def from_sibling(h, k):
        def one(zz, carry):
            ctx_copy(h, k, zz * 2 + 1 - c, 2, dev_sib).wait_recv()
            return carry

        lax.fori_loop(0, NZ, one, 0)

    n_col = lax.broadcasted_iota(jnp.int32, (QROWS, 256), 1)
    n_pos = (n_col // 16) * 64 + 2 * (n_col % 16)

    def attend(h, k):
        even = ctx[h, k, :, :, 0:KVR].reshape(256, KVR)
        odd = ctx[h, k, :, :, KVR : 2 * KVR].reshape(256, KVR)
        rope = ctx[h, k, :, :, 2 * KVR : PACK].reshape(256, 128)
        query = qn[k]
        rope_scores = nt_dot(qr[k], rope)
        length = ctx_len[k]
        pos = n_pos + h * 32
        s_even = (nt_dot(query, even) + rope_scores[:QROWS]) * softmax_scale
        s_odd = (nt_dot(query, odd) + rope_scores[QROWS:]) * softmax_scale
        s_even = jnp.where(pos < length, s_even, -jnp.inf)
        s_odd = jnp.where(pos + 1 < length, s_odd, -jnp.inf)
        old = m_s[k]
        top = jnp.maximum(old, jnp.max(jnp.maximum(s_even, s_odd), axis=1, keepdims=True))
        fade = jnp.exp(old - top)
        p_even = jnp.exp(s_even - top)
        p_odd = jnp.exp(s_odd - top)
        m_s[k] = top
        l_s[k] = l_s[k] * fade + jnp.sum(p_even + p_odd, axis=1, keepdims=True)
        acc_s[k] = acc_s[k] * fade + (nn_dot(p_even.astype(BF16), even) + nn_dot(p_odd.astype(BF16), odd))

    open_half(0)
    for i in range(1, HOP_A + 1):
        hop(0, i)
        if i == 2:
            open_half(1)
    for i in range(1, HOP_A + 1):
        hop(1, i)
        if i < HOP_A:
            from_sibling(0, i - 1)
            attend(0, i - 1)

    def finish(k, carry):
        from_sibling(1, k)
        attend(1, k)
        rows = (acc_s[k] / l_s[k]).astype(BF16)
        at = pl.ds(pl.multiple_of(k * 32, 32), 32)
        for h in range(HEADS):
            att[h, at, :] = rows[h * 32 : (h + 1) * 32]
        return carry

    lax.fori_loop(0, REQ, finish, 0)

    local[1].wait()
    for h in range(HEADS):
        hvbuf[c, :, h * 128 : (h + 1) * 128] = nn_dot(att[h], wuv[:, h * 128 : (h + 1) * 128]).astype(BF16)
    hv_copy = pltpu.make_async_remote_copy(
        src_ref=hvbuf.at[c], dst_ref=hvbuf.at[c], send_sem=hv_send, recv_sem=hv_recv,
        device_id=dev_sib, device_id_type=MESH,
    )
    hv_arrive = pltpu.make_async_remote_copy(
        src_ref=hvbuf.at[1 - c], dst_ref=hvbuf.at[1 - c], send_sem=hv_send, recv_sem=hv_recv,
        device_id=dev_sib, device_id_type=MESH,
    )
    hv_copy.start()
    local[2].wait()
    w_arrive.wait_recv()
    hv_arrive.wait_recv()

    def block_rows(zb):
        return pl.ds(pl.multiple_of((zb % 2) * BR, 16), BR)

    def partial(zb):
        rows = block_rows(zb)
        cols = pl.ds(pl.multiple_of((zb // 2) * BC, 128), BC)
        return nn_dot(hvbuf[0, rows, :], wout[0, :, cols]) + nn_dot(hvbuf[1, rows, :], wout[1, :, cols])

    def push_a(i):
        return pltpu.make_async_remote_copy(
            src_ref=snd_a.at[i], dst_ref=rcv_a.at[i], send_sem=ra_send.at[i], recv_sem=ra_recv.at[i],
            device_id=dev_a, device_id_type=MESH,
        )

    def push_b(i):
        return pltpu.make_async_remote_copy(
            src_ref=snd_b.at[i], dst_ref=rcv_b.at[i], send_sem=rb_send.at[i], recv_sem=rb_recv.at[i],
            device_id=dev_b, device_id_type=MESH,
        )

    snd_a[0] = partial(ring(HOP_A)).astype(BF16)
    push_a(0).start()
    snd_b[0] = partial(ring(-HOP_B)).astype(BF16)
    push_b(0).start()

    def reduce_step(i, carry):
        term = partial(ring(HOP_A - i))
        push_a(i - 1).wait_recv()
        snd_a[i] = (term + rcv_a[i - 1].astype(F32)).astype(BF16)
        push_a(i).start()

        @pl.when(i < HOP_B)
        def _():
            term_b = partial(ring(i - HOP_B))
            push_b(i - 1).wait_recv()
            snd_b[i] = (term_b + rcv_b[i - 1].astype(F32)).astype(BF16)
            push_b(i).start()

        return carry

    lax.fori_loop(1, HOP_A, reduce_step, 0)
    own = partial(z)
    push_b(HOP_B - 1).wait_recv()
    own = own + rcv_b[HOP_B - 1].astype(F32)
    push_a(HOP_A - 1).wait_recv()
    own = own + rcv_a[HOP_A - 1].astype(F32)

    def hid_copy(zb, way, device):
        return pltpu.make_async_remote_copy(
            src_ref=hid.at[c, zb], dst_ref=hid.at[c, zb], send_sem=h_send.at[zb, way],
            recv_sem=h_recv.at[c, zb], device_id=device, device_id_type=MESH,
        )

    def hid_sibling(zb):
        return pltpu.make_async_remote_copy(
            src_ref=hid.at[1 - c, zb], dst_ref=hid.at[1 - c, zb], send_sem=h_send.at[zb, 2],
            recv_sem=h_recv.at[1 - c, zb], device_id=dev_sib, device_id_type=MESH,
        )

    lg[...] = jnp.zeros_like(lg)
    ss[...] = jnp.zeros_like(ss)

    def use(core, zb):
        rows = block_rows(zb)
        x = hid[core, zb]
        depth = pl.ds(pl.multiple_of(core * HALF + (zb // 2) * BC, 128), BC)
        lg[rows, :] += nn_dot(x, wvoc[depth, :])
        wide = x.astype(F32)
        square = wide * wide
        total = square[:, 0:128]
        for j in range(1, BC // 128):
            total = total + square[:, j * 128 : (j + 1) * 128]
        ss[rows, :] += total

    hid[c, z] = own.astype(BF16)
    hid_copy(z, 0, dev_a).start()
    hid_copy(z, 1, dev_b).start()
    hid_copy(z, 2, dev_sib).start()
    local[3].wait()
    use(c, z)

    def gather_step(i, carry):
        za = ring(-i)
        hid_copy(za, 0, dev_a).wait_recv()

        @pl.when(i < HOP_A)
        def _():
            hid_copy(za, 0, dev_a).start()

        hid_copy(za, 2, dev_sib).start()

        @pl.when(i <= HOP_B)
        def _():
            zb = ring(i)
            hid_copy(zb, 1, dev_b).wait_recv()

            @pl.when(i < HOP_B)
            def _():
                hid_copy(zb, 1, dev_b).start()

            hid_copy(zb, 2, dev_sib).start()
            use(c, zb)

        use(c, za)
        back = ring(i - 1)
        hid_sibling(back).wait_recv()
        use(1 - c, back)

        @pl.when(i > 1)
        def _():
            ahead = ring(1 - i)
            hid_sibling(ahead).wait_recv()
            use(1 - c, ahead)

        return carry

    lax.fori_loop(1, HOP_A + 1, gather_step, 0)
    last = ring(HOP_A)
    hid_sibling(last).wait_recv()
    use(1 - c, last)

    lane = lax.broadcasted_iota(jnp.int32, (ROWS, 128), 1)
    wide_targets = jnp.concatenate(
        [target_ref[...].astype(F32), jnp.zeros((REQ, 96), F32)], axis=1
    )
    wide_targets = jnp.concatenate([wide_targets, jnp.zeros((8 - REQ, 128), F32)], axis=0)
    turned = jnp.transpose(jnp.concatenate([wide_targets] * 16, axis=0))
    target_col = jnp.concatenate([turned[0:32, k : k + 1] for k in range(REQ)], axis=0).astype(jnp.int32)
    factor = lax.rsqrt(jnp.sum(ss[...], axis=1, keepdims=True) * (1.0 / D) + norm_epsilon)
    logits = lg[...] * factor
    top = jnp.max(logits, axis=1, keepdims=True)
    total = jnp.sum(jnp.exp(logits - top), axis=1, keepdims=True)
    hit = lax.broadcasted_iota(jnp.int32, (ROWS, VOCAB_LOCAL), 1) == target_col - t * VOCAB_LOCAL
    aimed = jnp.sum(jnp.where(hit, logits, 0.0), axis=1, keepdims=True)
    table = jnp.where(lane == 0, top, jnp.where(lane == 1, total, jnp.where(lane == 2, aimed, 0.0)))
    table = jnp.concatenate([table, jnp.zeros((128 - ROWS, 128), F32)], axis=0)
    stat[t] = jnp.transpose(table)[0:8, :]

    def stat_copy(d):
        return pltpu.make_async_remote_copy(
            src_ref=stat.at[t], dst_ref=stat.at[t], send_sem=st_send.at[d], recv_sem=st_recv.at[t],
            device_id={"tp": lax.rem(t + d, NT)}, device_id_type=MESH,
        )

    def stat_arrive(d):
        peer = lax.rem(t + d, NT)
        return pltpu.make_async_remote_copy(
            src_ref=stat.at[peer], dst_ref=stat.at[peer], send_sem=st_send.at[d], recv_sem=st_recv.at[peer],
            device_id={"tp": peer}, device_id_type=MESH,
        )

    for d in range(1, NT):
        stat_copy(d).start()

    def drain_ctx(index, carry):
        h, k = index // REQ, index % REQ
        for i in range(HOP_A):
            ctx_copy(h, k, ring(-i) * 2 + c, 0, dev_a).wait_send()
        for i in range(HOP_B):
            ctx_copy(h, k, ring(i) * 2 + c, 1, dev_b).wait_send()
        for zz in range(NZ):
            ctx_copy(h, k, zz * 2 + c, 2, dev_sib).wait_send()
        return carry

    lax.fori_loop(0, 2 * REQ, drain_ctx, 0)
    for h in range(2):
        for k in range(NG):
            route(h, k).wait_send()
    w_copy.wait_send()
    hv_copy.wait_send()
    for i in range(HOP_A):
        push_a(i).wait_send()
        hid_copy(ring(-i), 0, dev_a).wait_send()
    for i in range(HOP_B):
        push_b(i).wait_send()
        hid_copy(ring(i), 1, dev_b).wait_send()
    for zz in range(NZ):
        hid_copy(zz, 2, dev_sib).wait_send()

    lane1 = lax.broadcasted_iota(jnp.int32, (1, 128), 1)
    length = jnp.ones((1, 128), jnp.int32)
    for k in range(REQ):
        for a in range(CAND):
            length = jnp.where(lane1 // STEPS == k * CAND + a, reply_len[k, a], length)

    for d in range(1, NT):
        stat_arrive(d).wait_recv()
    every = [stat[d] for d in range(NT)]
    joint = functools.reduce(jnp.maximum, [one[0:1] for one in every])
    joint_total = functools.reduce(jnp.add, [one[1:2] * jnp.exp(one[0:1] - joint) for one in every])
    joint_aimed = functools.reduce(jnp.add, [one[2:3] for one in every])
    log_prob = joint_aimed - (joint + jnp.log(joint_total))
    inside = jnp.logical_and(lane1 % STEPS < length, lane1 < ROWS)
    value = jnp.where(inside, log_prob, 0.0) / length.astype(F32)
    spread = jnp.where(
        lax.broadcasted_iota(jnp.int32, (8, 128), 1) // 32 == lax.broadcasted_iota(jnp.int32, (8, 128), 0),
        jnp.broadcast_to(value, (8, 128)),
        0.0,
    )
    source_lane = lax.broadcasted_iota(jnp.int32, (128, 128), 0)
    pick = ((source_lane % 32) // STEPS == lax.broadcasted_iota(jnp.int32, (128, 128), 1)).astype(F32)
    summed = lax.dot_general(
        spread, pick, (((1,), (0,)), ((), ())), precision=lax.Precision.HIGHEST, preferred_element_type=F32
    )
    score_ref[...] = summed[0:REQ, 0:CAND]
    for d in range(1, NT):
        stat_copy(d).wait_send()


def per_device(
    ctx_latent, ctx_rope, ctx_scale, dest, ctx_len, queries, reply_keys, reply_len, targets, w_uv, w_out, w_vocab
):
    vmem = pl.BlockSpec(memory_space=pltpu.VMEM)
    smem = pl.BlockSpec(memory_space=pltpu.SMEM)
    hbm = pl.BlockSpec(memory_space=pl.ANY)
    dma = pltpu.SemaphoreType.DMA
    return pl.pallas_call(
        kernel,
        out_shape=jax.ShapeDtypeStruct((REQ, CAND), F32),
        in_specs=[smem, smem, smem, vmem, vmem, vmem, vmem, vmem, hbm, hbm, hbm, hbm],
        out_specs=vmem,
        scratch_shapes=[
            pltpu.VMEM((REQ, 2, 16, PACK), BF16),
            pltpu.VMEM((2, NG, 2, 16, PACK), BF16),
            pltpu.VMEM((NG * 2, 16, PACK), BF16),
            pltpu.VMEM((NG * 2, 16, PACK), BF16),
            pltpu.VMEM((2, REQ, NT, 16, PACK), BF16),
            pltpu.VMEM((REQ, 32, HEADS * KEY), BF16),
            pltpu.VMEM((REQ, QROWS, KVR), BF16),
            pltpu.VMEM((REQ, 2 * QROWS, 128), BF16),
            pltpu.VMEM((32, KVR), BF16),
            pltpu.VMEM((32, 128), BF16),
            pltpu.VMEM((REQ, QROWS, 1), F32),
            pltpu.VMEM((REQ, QROWS, 1), F32),
            pltpu.VMEM((REQ, QROWS, KVR), F32),
            pltpu.VMEM((HEADS, ROWS, KVR), BF16),
            pltpu.VMEM((2, ROWS, 512), BF16),
            pltpu.VMEM((KVR, 512), BF16),
            pltpu.VMEM((2, 512, HALF), BF16),
            pltpu.VMEM((D, VOCAB_LOCAL), BF16),
            pltpu.VMEM((HOP_A, BR, BC), BF16),
            pltpu.VMEM((HOP_B, BR, BC), BF16),
            pltpu.VMEM((HOP_A, BR, BC), BF16),
            pltpu.VMEM((HOP_B, BR, BC), BF16),
            pltpu.VMEM((2, NZ, BR, BC), BF16),
            pltpu.VMEM((ROWS, VOCAB_LOCAL), F32),
            pltpu.VMEM((ROWS, 128), F32),
            pltpu.VMEM((NT, 8, 128), F32),
            dma((4,)),
            dma((2, NG)),
            dma((2, NG)),
            dma((2, REQ, NT, 3)),
            dma((2, REQ, NT)),
            dma, dma, dma, dma,
            dma((HOP_A,)), dma((HOP_A,)), dma((HOP_B,)), dma((HOP_B,)),
            dma((NZ, 3)), dma((2, NZ)),
            dma((NT,)), dma((NT,)),
        ],
        compiler_params=pltpu.CompilerParams(
            collective_id=0, has_side_effects=True, vmem_limit_bytes=48 * 1024 * 1024
        ),
    )(
        dest, ctx_len, reply_len, ctx_latent, ctx_rope, ctx_scale, reply_keys, targets,
        queries, w_uv, w_out, w_vocab,
    )


def solution(mesh):
    group = ("section", "grp")
    placed = (
        P(group, "tp", None),
        P(group, "tp", None),
        P(group, "tp", None),
        P(),
        P(group),
        P(group, None, "tp"),
        P(group, None, None),
        P(group, None),
        P(group, None),
        P(None, "tp"),
        P("tp", None),
        P(None, "tp"),
    )
    return jax.shard_map(
        per_device, mesh=mesh, in_specs=placed, out_specs=P(group, None), check_vma=False
    )
```

```python
import functools

import jax
import jax.numpy as jnp
from jax import lax
from jax.experimental import pallas as pl
from jax.experimental.pallas import tpu as pltpu
from jax.sharding import PartitionSpec as P

MESH = pl.DeviceIdType.MESH
BF16, F32 = jnp.bfloat16, jnp.float32

softmax_scale = 192.0 ** (-0.5)
norm_epsilon = 1e-06

NS, NG, NZ, NT = 4, 4, 8, 16
REQ, CAND, STEPS, HEADS = 3, 8, 4, 4
KVR, ROPE, KEY = 512, 64, 576
ROWS = REQ * CAND * STEPS
QROWS = HEADS * CAND * STEPS
D, HALF = 7168, 3584
BR, BC = 48, 896
HOP_A, HOP_B = 4, 3
WIDE_A, WIDE_B = 640, 512
CHUNKS = 4
VOCAB_LOCAL = 256
ROUTE, USE = -1, -2
SCHEDULE = (
    (1, ROUTE), (0, 0), (2, ROUTE), (1, 0), (0, 1), (3, ROUTE), (2, 0), (1, 1), (0, 2), (3, 0), (2, 1), (1, 2), (0, 3),
    (3, 1), (2, 2), (1, 3), (0, 4), (3, 2), (2, 3), (1, 4), (0, USE), (3, 3), (2, 4), (1, USE), (3, 4), (2, USE), (3, USE),
)


def nt_dot(a, b):
    return lax.dot_general(a, b, (((1,), (1,)), ((), ())), preferred_element_type=F32)


def nn_dot(a, b):
    return lax.dot_general(a, b, (((1,), (0,)), ((), ())), preferred_element_type=F32)


def unpack_key(slab, index):
    n = slab.shape[0]
    low = lax.broadcasted_iota(jnp.int32, (n, 128), 1) < ROPE
    start = index * KEY
    first = start // 128
    if index % 2 == 0:
        latent = slab[:, start : start + KVR]
        tile = slab[:, start + KVR : start + KVR + 128]
        rope_low = jnp.where(low, tile, 0.0)
        rope_high = pltpu.roll(rope_low, 64, 1)
    else:
        turned = [
            pltpu.roll(slab[:, (first + j) * 128 : (first + j + 1) * 128], 64, 1) for j in range(5)
        ]
        latent = jnp.concatenate([jnp.where(low, turned[j], turned[j + 1]) for j in range(4)], axis=1)
        rope_low = jnp.where(low, turned[4], 0.0)
        rope_high = pltpu.roll(rope_low, 64, 1)
    return latent, rope_low, rope_high


def kernel(
    dest_hbm, ctx_len_hbm, reply_len_hbm, lat_hbm, rope_hbm, scale_hbm, reply_hbm, target_hbm,
    query_hbm, uv_hbm, out_hbm, vocab_hbm,
    score_ref,
    dest, ctx_len, reply_len, lat_ref, rope_ref, scale_ref, reply_ref, target_ref, xsrc_a, xsrc_b, sbuf_a, sbuf_b, rbuf_0, rbuf_1, rbuf_2, rbuf_3, ctx_a, ctx_b, q_in, qn, qr, rkn, rkr, m_s, l_s, acc_s, att, hvbuf, wuv, wout, wvoc,
    part, snd, rcv, hid, lg, ss, stat,
    local_sem, route_send, route_recv, ctx_send, ctx_recv, w_send, w_recv, hv_send, hv_recv,
    r_send, r_recv, h_send, h_recv, st_send, st_recv,
):
    s, g, t = lax.axis_index("section"), lax.axis_index("grp"), lax.axis_index("tp")
    z, c = t // 2, t % 2
    sib = t + 1 - 2 * c
    sgn = 1 - 2 * c
    xsrc, sbuf, ctx = (xsrc_a, xsrc_b), (sbuf_a, sbuf_b), (ctx_a, ctx_b)
    rbuf = (rbuf_0, rbuf_1, rbuf_2, rbuf_3)
    next_s = lax.rem(s + 1, NS)
    prev_s = lax.rem(s + NS - 1, NS)

    def ring(step):
        return lax.rem(z + sgn * step + 2 * NZ, NZ)

    dev_a, dev_b = {"tp": ring(1) * 2 + c}, {"tp": ring(-1) * 2 + c}
    dev_a2, dev_b2 = {"tp": ring(2) * 2 + c}, {"tp": ring(-2) * 2 + c}
    dev_sib = {"tp": sib}

    barrier = pltpu.get_barrier_semaphore()
    for k in range(NG):
        pl.semaphore_signal(barrier, inc=1, device_id={"section": prev_s, "grp": k}, device_id_type=MESH)
    for device in (dev_a, dev_b, dev_a2, dev_b2, dev_sib):
        pl.semaphore_signal(barrier, inc=1, device_id=device, device_id_type=MESH)

    own_cols = pl.ds(pl.multiple_of(c * HALF, 128), HALF)
    other_cols = pl.ds(pl.multiple_of((1 - c) * HALF, 128), HALF)
    pairs = [
        (scale_hbm, scale_ref), (lat_hbm, lat_ref), (rope_hbm, rope_ref), (dest_hbm, dest),
        (query_hbm, q_in), (reply_hbm, reply_ref), (ctx_len_hbm, ctx_len),
        (uv_hbm, wuv), (out_hbm.at[:, own_cols], wout.at[c]), (vocab_hbm, wvoc),
        (target_hbm, target_ref), (reply_len_hbm, reply_len),
    ]
    local = [pltpu.make_async_copy(a, b, local_sem.at[i]) for i, (a, b) in enumerate(pairs)]
    for copy in local:
        copy.start()

    row = lax.broadcasted_iota(jnp.int32, (64, 64), 0)
    col = lax.broadcasted_iota(jnp.int32, (64, 64), 1)
    place = 2 * ((row // 32) * 16 + row % 16) + (row // 16) % 2
    perm = (col == place).astype(BF16)
    for copy in local[:4]:
        copy.wait()
    scales = jnp.concatenate([scale_ref[j].astype(F32) for j in range(REQ)] + [jnp.zeros((4, 64), F32)], axis=0)
    scales = jnp.concatenate([scales, jnp.zeros((16, 64), F32)], axis=1)
    scales = jnp.transpose(jnp.concatenate([scales] * 8, axis=0))
    for j in range(REQ):
        parts = [
            (lat_ref[j, :, b * 128 : (b + 1) * 128].astype(F32) * scales[0:64, j * 4 + b : j * 4 + b + 1]).astype(BF16)
            for b in range(4)
        ]
        moved = nn_dot(perm, jnp.concatenate(parts, axis=1)).astype(BF16)
        for h in range(2):
            xsrc_a[j, h, :, 0:KVR] = moved[h * 32 : h * 32 + 16]
            xsrc_a[j, h, :, KVR:WIDE_A] = rope_ref[j, h * 16 : (h + 1) * 16, :]
            xsrc_b[j, h] = moved[h * 32 + 16 : h * 32 + 32]

    own_dest = [dest[(s * NG + g) * REQ + j] for j in range(REQ)]
    for h in range(CHUNKS):
        for k in range(NG):
            first = jnp.where(own_dest[0] == k, 0, jnp.where(own_dest[1] == k, 1, 2))
            last = jnp.where(own_dest[2] == k, 2, jnp.where(own_dest[1] == k, 1, 0))
            sbuf[h % 2][h // 2, k, 0] = xsrc[h % 2][first, h // 2]
            sbuf[h % 2][h // 2, k, 1] = xsrc[h % 2][last, h // 2]

    pl.semaphore_wait(barrier, NG + 5)

    def route(h, j):
        k = lax.rem(g + j, NG)
        return pltpu.make_async_remote_copy(
            src_ref=sbuf[h % 2].at[h // 2, k], dst_ref=rbuf[h].at[pl.ds(2 * g, 2)],
            send_sem=route_send.at[h, j], recv_sem=route_recv.at[h, g],
            device_id={"section": next_s, "grp": k}, device_id_type=MESH,
        )

    def route_arrived(h, k):
        return pltpu.make_async_remote_copy(
            src_ref=sbuf[h % 2].at[h // 2, k], dst_ref=rbuf[h].at[pl.ds(2 * k, 2)],
            send_sem=route_send.at[h, k], recv_sem=route_recv.at[h, k],
            device_id={"section": next_s, "grp": k}, device_id_type=MESH,
        )

    def route_start(h):
        for k in range(NG):
            route(h, k).start()

    def route_left(h):
        for k in range(NG):
            route(h, k).wait_send()

    route_start(0)
    w_copy = pltpu.make_async_remote_copy(
        src_ref=out_hbm.at[:, other_cols], dst_ref=wout.at[c],
        send_sem=w_send, recv_sem=w_recv, device_id=dev_sib, device_id_type=MESH,
    )
    w_arrive = pltpu.make_async_remote_copy(
        src_ref=out_hbm.at[:, other_cols], dst_ref=wout.at[1 - c],
        send_sem=w_send, recv_sem=w_recv, device_id=dev_sib, device_id_type=MESH,
    )

    def drain_route():
        route_left(CHUNKS - 1)
        w_copy.wait_send()

    picks = [jnp.int32(0)] * REQ
    count = jnp.int32(0)
    for h in range(NG):
        seen = jnp.int32(0)
        for j in range(REQ):
            hit = dest[(prev_s * NG + h) * REQ + j] == g
            for k in range(REQ):
                picks[k] = jnp.where(jnp.logical_and(hit, count == k), h * 2 + seen, picks[k])
            one = jnp.where(hit, 1, 0)
            seen = seen + one
            count = count + one
    picks = [jnp.minimum(pick, 2 * NG - 1) for pick in picks]

    for copy in local[4:7]:
        copy.wait()
    a_row = (lax.broadcasted_iota(jnp.int32, (QROWS, 32), 0) % 32) // STEPS
    t_row = lax.broadcasted_iota(jnp.int32, (QROWS, 32), 0) % STEPS
    a_col = lax.broadcasted_iota(jnp.int32, (QROWS, 32), 1) % CAND
    u_col = lax.broadcasted_iota(jnp.int32, (QROWS, 32), 1) // CAND
    reply_seen = jnp.logical_and(a_row == a_col, u_col <= t_row)

    def prepare(k, carry):
        slab = q_in[k].astype(F32)
        for h in range(HEADS):
            latent, low, high = unpack_key(slab, h)
            qn[k, h * 32 : (h + 1) * 32, :] = latent.astype(BF16)
            qr[k, h * 32 : (h + 1) * 32, :] = low.astype(BF16)
            qr[k, QROWS + h * 32 : QROWS + (h + 1) * 32, :] = high.astype(BF16)
        keys = reply_ref[k].astype(F32)
        pieces = [unpack_key(keys, u) for u in range(STEPS)]
        rkn[...] = jnp.concatenate([piece[0] for piece in pieces], axis=0).astype(BF16)
        rkr[...] = jnp.concatenate([piece[1] for piece in pieces], axis=0).astype(BF16)
        scores = nt_dot(qn[k], rkn[...]) + nt_dot(qr[k, 0:QROWS], rkr[...])
        scores = jnp.where(reply_seen, scores * softmax_scale, -jnp.inf)
        top = jnp.max(scores, axis=1, keepdims=True)
        weight = jnp.exp(scores - top)
        m_s[k] = top
        l_s[k] = jnp.sum(weight, axis=1, keepdims=True)
        acc_s[k] = nn_dot(weight.astype(BF16), rkn[...])
        return carry

    lax.fori_loop(0, REQ, prepare, 0)

    def ctx_copy(h, slot, way, device):
        block = ctx[h % 2].at[h // 2, slot]
        return pltpu.make_async_remote_copy(
            src_ref=block, dst_ref=block, send_sem=ctx_send.at[h, slot, way], recv_sem=ctx_recv.at[h, slot],
            device_id=device, device_id_type=MESH,
        )

    ctx_ways = (dev_a, dev_b, dev_sib)

    def open_chunk(h):
        for k in range(NG):
            route_arrived(h, k).wait_recv()
        for k in range(REQ):
            ctx[h % 2][h // 2, t, k] = rbuf[h][picks[k]]
        for way in range(3):
            ctx_copy(h, t, way, ctx_ways[way]).start()

    def share(h, slot, *onward):
        ctx_copy(h, slot, 0, dev_a).wait_recv()
        for way in onward:
            ctx_copy(h, slot, way, ctx_ways[way]).start()
        ctx_copy(h, slot, 2, dev_sib).start()

    def hop(h, i):
        share(h, ring(-i) * 2 + c, *((0,) if i < HOP_A else ()))
        if i <= HOP_B:
            share(h, ring(i) * 2 + c, *((1,) if i < HOP_B else ()))

    n_col = lax.broadcasted_iota(jnp.int32, (QROWS, 256), 1)
    n_pos = (n_col // 16) * 64 + 2 * (n_col % 16)

    def attend(h, k):
        if h % 2 == 0:
            latent = ctx_a[h // 2, :, k, :, 0:KVR].reshape(256, KVR)
            rope_query = qr[k, 0:QROWS]
        else:
            latent = ctx_b[h // 2, :, k].reshape(256, KVR)
            rope_query = qr[k, QROWS : 2 * QROWS]
        rope = ctx_a[h // 2, :, k, :, KVR:WIDE_A].reshape(256, 128)
        scores = (nt_dot(qn[k], latent) + nt_dot(rope_query, rope)) * softmax_scale
        scores = jnp.where(n_pos + (h // 2) * 32 + h % 2 < ctx_len[k], scores, -jnp.inf)
        old = m_s[k]
        top = jnp.maximum(old, jnp.max(scores, axis=1, keepdims=True))
        fade = jnp.exp(old - top)
        weight = jnp.exp(scores - top)
        m_s[k] = top
        l_s[k] = l_s[k] * fade + jnp.sum(weight, axis=1, keepdims=True)
        acc_s[k] = acc_s[k] * fade + nn_dot(weight.astype(BF16), latent)

    def close_chunk(h):
        def one(zz, carry):
            ctx_copy(h, zz * 2 + 1 - c, 2, dev_sib).wait_recv()
            return carry

        lax.fori_loop(0, NZ, one, 0)

    for h, i in SCHEDULE:
        if i == ROUTE:
            route_left(h - 1)
            route_start(h)
            if h == CHUNKS - 1:
                w_copy.start()
        elif i == USE:
            close_chunk(h)
            for k in range(REQ):
                attend(h, k)
        elif i == 0:
            open_chunk(h)
        else:
            hop(h, i)
    for k in range(REQ):
        rows = (acc_s[k] / l_s[k]).astype(BF16)
        for h in range(HEADS):
            att[h, k * 32 : (k + 1) * 32, :] = rows[h * 32 : (h + 1) * 32]

    def drain_ctx():
        for h in range(CHUNKS):
            for i in range(HOP_A):
                ctx_copy(h, ring(-i) * 2 + c, 0, dev_a).wait_send()
            for i in range(HOP_B):
                ctx_copy(h, ring(i) * 2 + c, 1, dev_b).wait_send()
            for zz in range(NZ):
                ctx_copy(h, zz * 2 + c, 2, dev_sib).wait_send()

    local[7].wait()
    for h in range(HEADS):
        hvbuf[c, :, h * 128 : (h + 1) * 128] = nn_dot(att[h], wuv[:, h * 128 : (h + 1) * 128]).astype(BF16)
    hv_copy = pltpu.make_async_remote_copy(
        src_ref=hvbuf.at[c], dst_ref=hvbuf.at[c], send_sem=hv_send, recv_sem=hv_recv,
        device_id=dev_sib, device_id_type=MESH,
    )
    hv_arrive = pltpu.make_async_remote_copy(
        src_ref=hvbuf.at[1 - c], dst_ref=hvbuf.at[1 - c], send_sem=hv_send, recv_sem=hv_recv,
        device_id=dev_sib, device_id_type=MESH,
    )
    hv_copy.start()
    local[8].wait()
    w_arrive.wait_recv()
    hv_arrive.wait_recv()

    def block_rows(zb):
        return pl.ds(pl.multiple_of((zb // 4) * BR, 16), BR)

    def partials(index, zb):
        cols = pl.ds(pl.multiple_of((zb % 4) * BC, 128), BC)
        both = nn_dot(hvbuf[0], wout[0, :, cols]) + nn_dot(hvbuf[1], wout[1, :, cols])
        part[index, 0] = both[0:BR]
        part[index, 1] = both[BR : 2 * BR]

    targets_of = (dev_a2, dev_a, dev_b, dev_a, dev_b, dev_a2, dev_b2)

    def push(i):
        return pltpu.make_async_remote_copy(
            src_ref=snd.at[i], dst_ref=rcv.at[i], send_sem=r_send.at[i], recv_sem=r_recv.at[i],
            device_id=targets_of[i], device_id_type=MESH,
        )

    def send(i, value):
        snd[i] = value.astype(BF16)
        push(i).start()

    def received(i):
        push(i).wait_recv()
        return rcv[i].astype(F32)

    far, side, back = ring(4), ring(3), ring(-3)
    near_a, near_b, mid_a, mid_b = ring(1), ring(-1), ring(2), ring(-2)
    partials(0, far)
    send(0, part[0, far // 4])
    partials(1, side)
    send(1, part[1, side // 4])
    partials(2, back)
    send(2, part[2, back // 4])
    send(3, part[2, near_a // 4])
    send(4, part[1, near_b // 4])
    partials(3, mid_a)
    send(5, part[3, mid_a // 4] + received(0) + received(1))
    send(6, part[3, mid_b // 4] + received(2))
    own = part[0, z // 4] + received(3) + received(4)
    own = own + received(6)
    own = own + received(5)

    def drain_reduce():
        hv_copy.wait_send()
        for i in range(7):
            push(i).wait_send()

    ways = (dev_a, dev_a2, dev_b, dev_b2, dev_sib)

    def hid_copy(zb, way):
        return pltpu.make_async_remote_copy(
            src_ref=hid.at[c, zb], dst_ref=hid.at[c, zb], send_sem=h_send.at[zb, way],
            recv_sem=h_recv.at[c, zb], device_id=ways[way], device_id_type=MESH,
        )

    def hid_sibling(zb):
        return pltpu.make_async_remote_copy(
            src_ref=hid.at[1 - c, zb], dst_ref=hid.at[1 - c, zb], send_sem=h_send.at[zb, 4],
            recv_sem=h_recv.at[1 - c, zb], device_id=dev_sib, device_id_type=MESH,
        )

    lg[...] = jnp.zeros_like(lg)
    ss[...] = jnp.zeros_like(ss)

    def use(core, zb):
        rows = block_rows(zb)
        x = hid[core, zb]
        depth = pl.ds(pl.multiple_of(core * HALF + (zb % 4) * BC, 128), BC)
        lg[rows, :] += nn_dot(x, wvoc[depth, :])
        wide = x.astype(F32)
        square = wide * wide
        total = square[:, 0:128]
        for j in range(1, BC // 128):
            total = total + square[:, j * 128 : (j + 1) * 128]
        ss[rows, :] += total

    hid[c, z] = own.astype(BF16)
    for way in (1, 3, 0, 2, 4):
        hid_copy(z, way).start()
    local[9].wait()
    use(c, z)

    def take(zb, onward):
        hid_copy(zb, 0).wait_recv()
        for way in onward:
            hid_copy(zb, way).start()
        hid_copy(zb, 4).start()

    def use_sibling(zb):
        hid_sibling(zb).wait_recv()
        use(1 - c, zb)

    use_sibling(z)
    take(ring(-2), (1, 0))
    take(ring(2), (2,))
    use(c, ring(-2))
    use(c, ring(2))
    take(ring(-1), ())
    take(ring(1), ())
    use(c, ring(-1))
    use(c, ring(1))
    for step in (2, -2, 1, -1):
        use_sibling(ring(step))
    take(ring(-3), ())
    take(ring(3), ())
    use(c, ring(-3))
    use(c, ring(3))
    take(ring(4), ())
    use(c, ring(4))
    for step in (3, -3, 4):
        use_sibling(ring(step))

    def drain_hidden():
        for way in range(4):
            hid_copy(z, way).wait_send()
        hid_copy(ring(-2), 0).wait_send()
        hid_copy(ring(-2), 1).wait_send()
        hid_copy(ring(2), 2).wait_send()
        for zz in range(NZ):
            hid_copy(zz, 4).wait_send()

    local[10].wait()
    lane = lax.broadcasted_iota(jnp.int32, (ROWS, 128), 1)
    wide_targets = jnp.concatenate(
        [target_ref[...].astype(F32), jnp.zeros((REQ, 96), F32)], axis=1
    )
    wide_targets = jnp.concatenate([wide_targets, jnp.zeros((8 - REQ, 128), F32)], axis=0)
    turned = jnp.transpose(jnp.concatenate([wide_targets] * 16, axis=0))
    target_col = jnp.concatenate([turned[0:32, k : k + 1] for k in range(REQ)], axis=0).astype(jnp.int32)
    factor = lax.rsqrt(jnp.sum(ss[...], axis=1, keepdims=True) * (1.0 / D) + norm_epsilon)
    logits = lg[...] * factor
    top = jnp.max(logits, axis=1, keepdims=True)
    total = jnp.sum(jnp.exp(logits - top), axis=1, keepdims=True)
    hit = lax.broadcasted_iota(jnp.int32, (ROWS, VOCAB_LOCAL), 1) == target_col - t * VOCAB_LOCAL
    aimed = jnp.sum(jnp.where(hit, logits, 0.0), axis=1, keepdims=True)
    table = jnp.where(lane == 0, top, jnp.where(lane == 1, total, jnp.where(lane == 2, aimed, 0.0)))
    table = jnp.concatenate([table, jnp.zeros((128 - ROWS, 128), F32)], axis=0)
    stat[t] = jnp.transpose(table)[0:8, :]

    def stat_copy(d):
        return pltpu.make_async_remote_copy(
            src_ref=stat.at[t], dst_ref=stat.at[t], send_sem=st_send.at[d], recv_sem=st_recv.at[t],
            device_id={"tp": lax.rem(t + d, NT)}, device_id_type=MESH,
        )

    def stat_arrive(d):
        peer = lax.rem(t + d, NT)
        return pltpu.make_async_remote_copy(
            src_ref=stat.at[peer], dst_ref=stat.at[peer], send_sem=st_send.at[d], recv_sem=st_recv.at[peer],
            device_id={"tp": peer}, device_id_type=MESH,
        )

    for d in range(1, NT):
        stat_copy(d).start()

    local[11].wait()
    lane1 = lax.broadcasted_iota(jnp.int32, (1, 128), 1)
    lengths = jnp.concatenate([reply_len[...].astype(F32), jnp.zeros((REQ, 120), F32)], axis=1)
    lengths = jnp.concatenate([lengths, jnp.zeros((8 - REQ, 128), F32)], axis=0)
    sub8 = lax.broadcasted_iota(jnp.int32, (8, 128), 0)
    lane8 = lax.broadcasted_iota(jnp.int32, (8, 128), 1)
    sub128 = lax.broadcasted_iota(jnp.int32, (128, 128), 0)
    lane128 = lax.broadcasted_iota(jnp.int32, (128, 128), 1)
    to_lanes = ((lane128 % 32) // STEPS == sub128).astype(BF16)
    lengths = jnp.where(lane8 // 32 == sub8, nn_dot(lengths.astype(BF16), to_lanes), 0.0)
    lengths = jnp.sum(lengths, axis=0, keepdims=True)
    lengths = jnp.where(lane1 < ROWS, lengths, 1.0)

    drain_route()
    drain_ctx()
    drain_reduce()
    drain_hidden()
    for d in range(1, NT):
        stat_arrive(d).wait_recv()
    every = [stat[d] for d in range(NT)]
    joint = functools.reduce(jnp.maximum, [one[0:1] for one in every])
    joint_total = functools.reduce(jnp.add, [one[1:2] * jnp.exp(one[0:1] - joint) for one in every])
    joint_aimed = functools.reduce(jnp.add, [one[2:3] for one in every])
    log_prob = joint_aimed - (joint + jnp.log(joint_total))
    inside = jnp.logical_and((lane1 % STEPS).astype(F32) < lengths, lane1 < ROWS)
    value = jnp.where(inside, log_prob, 0.0) / lengths
    spread = jnp.where(lane8 // 32 == sub8, jnp.broadcast_to(value, (8, 128)), 0.0)
    pick = ((sub128 % 32) // STEPS == lane128).astype(F32)
    summed = lax.dot_general(
        spread, pick, (((1,), (0,)), ((), ())), precision=lax.Precision.HIGHEST, preferred_element_type=F32
    )
    score_ref[...] = summed[0:REQ, 0:CAND]
    for d in range(1, NT):
        stat_copy(d).wait_send()


def per_device(
    ctx_latent, ctx_rope, ctx_scale, dest, ctx_len, queries, reply_keys, reply_len, targets, w_uv, w_out, w_vocab
):
    vmem = pl.BlockSpec(memory_space=pltpu.VMEM)
    smem = pltpu.SMEM
    hbm = pl.BlockSpec(memory_space=pltpu.HBM)
    dma = pltpu.SemaphoreType.DMA
    return pl.pallas_call(
        kernel,
        out_shape=jax.ShapeDtypeStruct((REQ, CAND), F32),
        in_specs=[hbm] * 12,
        out_specs=vmem,
        scratch_shapes=[
            smem((48,), jnp.int32),
            smem((REQ,), jnp.int32),
            pltpu.VMEM((REQ, CAND), jnp.int32),
            pltpu.VMEM((REQ, 64, KVR), BF16),
            pltpu.VMEM((REQ, 32, 128), BF16),
            pltpu.VMEM((REQ, 4, 64), BF16),
            pltpu.VMEM((REQ, CAND, STEPS * KEY), BF16),
            pltpu.VMEM((REQ, 32), jnp.int32),
            pltpu.VMEM((REQ, 2, 16, WIDE_A), BF16),
            pltpu.VMEM((REQ, 2, 16, WIDE_B), BF16),
            pltpu.VMEM((2, NG, 2, 16, WIDE_A), BF16),
            pltpu.VMEM((2, NG, 2, 16, WIDE_B), BF16),
            pltpu.VMEM((NG * 2, 16, WIDE_A), BF16),
            pltpu.VMEM((NG * 2, 16, WIDE_B), BF16),
            pltpu.VMEM((NG * 2, 16, WIDE_A), BF16),
            pltpu.VMEM((NG * 2, 16, WIDE_B), BF16),
            pltpu.VMEM((2, NT, REQ, 16, WIDE_A), BF16),
            pltpu.VMEM((2, NT, REQ, 16, WIDE_B), BF16),
            pltpu.VMEM((REQ, 32, HEADS * KEY), BF16),
            pltpu.VMEM((REQ, QROWS, KVR), BF16),
            pltpu.VMEM((REQ, 2 * QROWS, 128), BF16),
            pltpu.VMEM((32, KVR), BF16),
            pltpu.VMEM((32, 128), BF16),
            pltpu.VMEM((REQ, QROWS, 1), F32),
            pltpu.VMEM((REQ, QROWS, 1), F32),
            pltpu.VMEM((REQ, QROWS, KVR), F32),
            pltpu.VMEM((HEADS, ROWS, KVR), BF16),
            pltpu.VMEM((2, ROWS, 512), BF16),
            pltpu.VMEM((KVR, 512), BF16),
            pltpu.VMEM((2, 512, HALF), BF16),
            pltpu.VMEM((D, VOCAB_LOCAL), BF16),
            pltpu.VMEM((4, 2, BR, BC), F32),
            pltpu.VMEM((7, BR, BC), BF16),
            pltpu.VMEM((7, BR, BC), BF16),
            pltpu.VMEM((2, NZ, BR, BC), BF16),
            pltpu.VMEM((ROWS, VOCAB_LOCAL), F32),
            pltpu.VMEM((ROWS, 128), F32),
            pltpu.VMEM((NT, 8, 128), F32),
            dma((12,)),
            dma((CHUNKS, NG)),
            dma((CHUNKS, NG)),
            dma((CHUNKS, NT, 3)),
            dma((CHUNKS, NT)),
            dma, dma, dma, dma,
            dma((7,)), dma((7,)),
            dma((NZ, 5)), dma((2, NZ)),
            dma((NT,)), dma((NT,)),
        ],
        compiler_params=pltpu.CompilerParams(
            collective_id=0, has_side_effects=True, vmem_limit_bytes=62 * 1024 * 1024
        ),
    )(
        dest, ctx_len, reply_len, ctx_latent, ctx_rope, jnp.swapaxes(ctx_scale, 1, 2), reply_keys, targets,
        queries, w_uv, w_out, w_vocab,
    )


def solution(mesh):
    group = ("section", "grp")
    placed = (
        P(group, "tp", None),
        P(group, "tp", None),
        P(group, "tp", None),
        P(),
        P(group),
        P(group, None, "tp"),
        P(group, None, None),
        P(group, None),
        P(group, None),
        P(None, "tp"),
        P("tp", None),
        P(None, "tp"),
    )
    return jax.shard_map(
        per_device, mesh=mesh, in_specs=placed, out_specs=P(group, None), check_vma=False
    )
```

```python
import functools

import jax
import jax.numpy as jnp
from jax import lax
from jax.experimental import pallas as pl
from jax.experimental.pallas import tpu as pltpu
from jax.sharding import PartitionSpec as P

MESH = pl.DeviceIdType.MESH
BF16, F32 = jnp.bfloat16, jnp.float32

softmax_scale = 192.0 ** (-0.5)
norm_epsilon = 1e-06

NS, NG, NZ, NT = 4, 4, 8, 16
REQ, CAND, STEPS, HEADS = 3, 8, 4, 4
KVR, ROPE, KEY = 512, 64, 576
ROWS = REQ * CAND * STEPS
QROWS = HEADS * CAND * STEPS
D, HALF = 7168, 3584
BR, BC = 48, 896
HOP_A, HOP_B = 4, 3
WIDE_A, WIDE_B = 640, 512
CHUNKS = 4
VOCAB_LOCAL = 256
ROUTE, USE = -1, -2
SCHEDULE = (
    (1, ROUTE), (0, 0), (2, ROUTE), (1, 0), (0, 1), (3, ROUTE), (2, 0), (1, 1), (0, 2), (3, 0), (2, 1), (1, 2), (0, 3),
    (3, 1), (2, 2), (1, 3), (0, 4), (3, 2), (2, 3), (1, 4), (0, USE), (3, 3), (2, 4), (1, USE), (2, USE), (3, 4), (3, USE),
)


def nt_dot(a, b):
    return lax.dot_general(a, b, (((1,), (1,)), ((), ())), preferred_element_type=F32)


def nn_dot(a, b):
    return lax.dot_general(a, b, (((1,), (0,)), ((), ())), preferred_element_type=F32)


def unpack_key(slab, index):
    n = slab.shape[0]
    low = lax.broadcasted_iota(jnp.int32, (n, 128), 1) < ROPE
    start = index * KEY
    first = start // 128
    if index % 2 == 0:
        latent = slab[:, start : start + KVR]
        tile = slab[:, start + KVR : start + KVR + 128]
        rope_low = jnp.where(low, tile, 0.0)
        rope_high = pltpu.roll(rope_low, 64, 1)
    else:
        turned = [
            pltpu.roll(slab[:, (first + j) * 128 : (first + j + 1) * 128], 64, 1) for j in range(5)
        ]
        latent = jnp.concatenate([jnp.where(low, turned[j], turned[j + 1]) for j in range(4)], axis=1)
        rope_low = jnp.where(low, turned[4], 0.0)
        rope_high = pltpu.roll(rope_low, 64, 1)
    return latent, rope_low, rope_high


def kernel(
    dest_hbm, ctx_len_hbm, reply_len_hbm, lat_hbm, rope_hbm, scale_hbm, reply_hbm, target_hbm,
    query_hbm, uv_hbm, out_hbm, vocab_hbm,
    score_ref,
    dest, ctx_len, reply_len, lat_ref, rope_ref, scale_ref, reply_ref, target_ref, xsrc_a, xsrc_b, sbuf_a, sbuf_b, rbuf_0, rbuf_1, rbuf_2, rbuf_3, ctx_a, ctx_b, q_in, qn, qr, rkn, rkr, m_s, l_s, acc_s, att, hvbuf, wuv, wout, wvoc,
    part, snd, rcv, hid, lg, ss, stat,
    local_sem, route_send, route_recv, ctx_send, ctx_recv, w_send, w_recv, hv_send, hv_recv,
    r_send, r_recv, h_send, h_recv, st_send, st_recv,
):
    s, g, t = lax.axis_index("section"), lax.axis_index("grp"), lax.axis_index("tp")
    z, c = t // 2, t % 2
    sib = t + 1 - 2 * c
    sgn = 1 - 2 * c
    xsrc, sbuf, ctx = (xsrc_a, xsrc_b), (sbuf_a, sbuf_b), (ctx_a, ctx_b)
    rbuf = (rbuf_0, rbuf_1, rbuf_2, rbuf_3)
    next_s = lax.rem(s + 1, NS)
    prev_s = lax.rem(s + NS - 1, NS)

    def ring(step):
        return lax.rem(z + sgn * step + 2 * NZ, NZ)

    dev_a, dev_b = {"tp": ring(1) * 2 + c}, {"tp": ring(-1) * 2 + c}
    dev_a2, dev_b2 = {"tp": ring(2) * 2 + c}, {"tp": ring(-2) * 2 + c}
    dev_sib = {"tp": sib}

    barrier = pltpu.get_barrier_semaphore()
    for k in range(NG):
        pl.semaphore_signal(barrier, inc=1, device_id={"section": prev_s, "grp": k}, device_id_type=MESH)
    for device in (dev_a, dev_b, dev_a2, dev_b2, dev_sib):
        pl.semaphore_signal(barrier, inc=1, device_id=device, device_id_type=MESH)

    own_cols = pl.ds(pl.multiple_of(c * HALF, 128), HALF)
    other_cols = pl.ds(pl.multiple_of((1 - c) * HALF, 128), HALF)
    pairs = [
        (scale_hbm, scale_ref), (lat_hbm, lat_ref), (rope_hbm, rope_ref), (dest_hbm, dest),
        (query_hbm, q_in), (reply_hbm, reply_ref), (ctx_len_hbm, ctx_len),
        (uv_hbm, wuv), (out_hbm.at[:, own_cols], wout.at[c]), (vocab_hbm, wvoc),
        (target_hbm, target_ref), (reply_len_hbm, reply_len),
    ]
    local = [pltpu.make_async_copy(a, b, local_sem.at[i]) for i, (a, b) in enumerate(pairs)]
    for copy in local:
        copy.start()

    row = lax.broadcasted_iota(jnp.int32, (64, 64), 0)
    col = lax.broadcasted_iota(jnp.int32, (64, 64), 1)
    place = 2 * ((row // 32) * 16 + row % 16) + (row // 16) % 2
    perm = (col == place).astype(BF16)
    for copy in local[:4]:
        copy.wait()
    scales = jnp.concatenate([scale_ref[j].astype(F32) for j in range(REQ)] + [jnp.zeros((4, 64), F32)], axis=0)
    scales = jnp.concatenate([scales, jnp.zeros((16, 64), F32)], axis=1)
    scales = jnp.transpose(jnp.concatenate([scales] * 8, axis=0))
    for j in range(REQ):
        parts = [
            (lat_ref[j, :, b * 128 : (b + 1) * 128].astype(F32) * scales[0:64, j * 4 + b : j * 4 + b + 1]).astype(BF16)
            for b in range(4)
        ]
        moved = nn_dot(perm, jnp.concatenate(parts, axis=1)).astype(BF16)
        for h in range(2):
            xsrc_a[j, h, :, 0:KVR] = moved[h * 32 : h * 32 + 16]
            xsrc_a[j, h, :, KVR:WIDE_A] = rope_ref[j, h * 16 : (h + 1) * 16, :]
            xsrc_b[j, h] = moved[h * 32 + 16 : h * 32 + 32]

    own_dest = [dest[(s * NG + g) * REQ + j] for j in range(REQ)]
    for h in range(CHUNKS):
        for k in range(NG):
            first = jnp.where(own_dest[0] == k, 0, jnp.where(own_dest[1] == k, 1, 2))
            last = jnp.where(own_dest[2] == k, 2, jnp.where(own_dest[1] == k, 1, 0))
            sbuf[h % 2][h // 2, k, 0] = xsrc[h % 2][first, h // 2]
            sbuf[h % 2][h // 2, k, 1] = xsrc[h % 2][last, h // 2]

    pl.semaphore_wait(barrier, NG + 5)

    def route(h, j):
        k = lax.rem(g + j, NG)
        return pltpu.make_async_remote_copy(
            src_ref=sbuf[h % 2].at[h // 2, k], dst_ref=rbuf[h].at[pl.ds(2 * g, 2)],
            send_sem=route_send.at[h, j], recv_sem=route_recv.at[h, g],
            device_id={"section": next_s, "grp": k}, device_id_type=MESH,
        )

    def route_arrived(h, k):
        return pltpu.make_async_remote_copy(
            src_ref=sbuf[h % 2].at[h // 2, k], dst_ref=rbuf[h].at[pl.ds(2 * k, 2)],
            send_sem=route_send.at[h, k], recv_sem=route_recv.at[h, k],
            device_id={"section": next_s, "grp": k}, device_id_type=MESH,
        )

    def route_start(h):
        for k in range(NG):
            route(h, k).start()

    def route_left(h):
        for k in range(NG):
            route(h, k).wait_send()

    route_start(0)
    w_copy = pltpu.make_async_remote_copy(
        src_ref=out_hbm.at[:, other_cols], dst_ref=wout.at[c],
        send_sem=w_send, recv_sem=w_recv, device_id=dev_sib, device_id_type=MESH,
    )
    w_arrive = pltpu.make_async_remote_copy(
        src_ref=out_hbm.at[:, other_cols], dst_ref=wout.at[1 - c],
        send_sem=w_send, recv_sem=w_recv, device_id=dev_sib, device_id_type=MESH,
    )

    def drain_route():
        route_left(CHUNKS - 1)
        w_copy.wait_send()

    picks = [jnp.int32(0)] * REQ
    count = jnp.int32(0)
    for h in range(NG):
        seen = jnp.int32(0)
        for j in range(REQ):
            hit = dest[(prev_s * NG + h) * REQ + j] == g
            for k in range(REQ):
                picks[k] = jnp.where(jnp.logical_and(hit, count == k), h * 2 + seen, picks[k])
            one = jnp.where(hit, 1, 0)
            seen = seen + one
            count = count + one
    picks = [jnp.minimum(pick, 2 * NG - 1) for pick in picks]

    for copy in local[4:7]:
        copy.wait()
    a_row = (lax.broadcasted_iota(jnp.int32, (QROWS, 32), 0) % 32) // STEPS
    t_row = lax.broadcasted_iota(jnp.int32, (QROWS, 32), 0) % STEPS
    a_col = lax.broadcasted_iota(jnp.int32, (QROWS, 32), 1) % CAND
    u_col = lax.broadcasted_iota(jnp.int32, (QROWS, 32), 1) // CAND
    reply_seen = jnp.logical_and(a_row == a_col, u_col <= t_row)

    def prepare(k, carry):
        slab = q_in[k].astype(F32)
        for h in range(HEADS):
            latent, low, high = unpack_key(slab, h)
            qn[k, h * 32 : (h + 1) * 32, :] = latent.astype(BF16)
            qr[k, h * 32 : (h + 1) * 32, :] = low.astype(BF16)
            qr[k, QROWS + h * 32 : QROWS + (h + 1) * 32, :] = high.astype(BF16)
        keys = reply_ref[k].astype(F32)
        pieces = [unpack_key(keys, u) for u in range(STEPS)]
        rkn[...] = jnp.concatenate([piece[0] for piece in pieces], axis=0).astype(BF16)
        rkr[...] = jnp.concatenate([piece[1] for piece in pieces], axis=0).astype(BF16)
        scores = nt_dot(qn[k], rkn[...]) + nt_dot(qr[k, 0:QROWS], rkr[...])
        scores = jnp.where(reply_seen, scores * softmax_scale, -jnp.inf)
        top = jnp.max(scores, axis=1, keepdims=True)
        weight = jnp.exp(scores - top)
        m_s[k] = top
        l_s[k] = jnp.sum(weight, axis=1, keepdims=True)
        acc_s[k] = nn_dot(weight.astype(BF16), rkn[...])
        return carry

    lax.fori_loop(0, REQ, prepare, 0)

    def ctx_copy(h, slot, way, device):
        block = ctx[h % 2].at[h // 2, slot]
        return pltpu.make_async_remote_copy(
            src_ref=block, dst_ref=block, send_sem=ctx_send.at[h, slot, way], recv_sem=ctx_recv.at[h, slot],
            device_id=device, device_id_type=MESH,
        )

    ctx_ways = (dev_a, dev_b, dev_sib)

    def open_chunk(h):
        for k in range(NG):
            route_arrived(h, k).wait_recv()
        for k in range(REQ):
            ctx[h % 2][h // 2, t, k] = rbuf[h][picks[k]]
        for way in range(3):
            ctx_copy(h, t, way, ctx_ways[way]).start()

    def share(h, slot, *onward):
        ctx_copy(h, slot, 0, dev_a).wait_recv()
        for way in onward:
            ctx_copy(h, slot, way, ctx_ways[way]).start()
        ctx_copy(h, slot, 2, dev_sib).start()

    def hop(h, i):
        share(h, ring(-i) * 2 + c, *((0,) if i < HOP_A else ()))
        if i <= HOP_B:
            share(h, ring(i) * 2 + c, *((1,) if i < HOP_B else ()))

    n_col = lax.broadcasted_iota(jnp.int32, (QROWS, 256), 1)
    n_pos = (n_col // 16) * 64 + 2 * (n_col % 16)

    def attend(h, k):
        if h % 2 == 0:
            latent = ctx_a[h // 2, :, k, :, 0:KVR].reshape(256, KVR)
            rope_query = qr[k, 0:QROWS]
        else:
            latent = ctx_b[h // 2, :, k].reshape(256, KVR)
            rope_query = qr[k, QROWS : 2 * QROWS]
        rope = ctx_a[h // 2, :, k, :, KVR:WIDE_A].reshape(256, 128)
        scores = (nt_dot(qn[k], latent) + nt_dot(rope_query, rope)) * softmax_scale
        scores = jnp.where(n_pos + (h // 2) * 32 + h % 2 < ctx_len[k], scores, -jnp.inf)
        old = m_s[k]
        top = jnp.maximum(old, jnp.max(scores, axis=1, keepdims=True))
        fade = jnp.exp(old - top)
        weight = jnp.exp(scores - top)
        m_s[k] = top
        l_s[k] = l_s[k] * fade + jnp.sum(weight, axis=1, keepdims=True)
        acc_s[k] = acc_s[k] * fade + nn_dot(weight.astype(BF16), latent)

    def close_chunk(h):
        def one(zz, carry):
            ctx_copy(h, zz * 2 + 1 - c, 2, dev_sib).wait_recv()
            return carry

        lax.fori_loop(0, NZ, one, 0)

    for h, i in SCHEDULE:
        if i == ROUTE:
            route_left(h - 1)
            route_start(h)
            if h == CHUNKS - 1:
                w_copy.start()
        elif i == USE:
            close_chunk(h)
            for k in range(REQ):
                attend(h, k)
        elif i == 0:
            open_chunk(h)
        else:
            hop(h, i)
    for k in range(REQ):
        rows = (acc_s[k] / l_s[k]).astype(BF16)
        for h in range(HEADS):
            att[h, k * 32 : (k + 1) * 32, :] = rows[h * 32 : (h + 1) * 32]

    def drain_ctx():
        for h in range(CHUNKS):
            for i in range(HOP_A):
                ctx_copy(h, ring(-i) * 2 + c, 0, dev_a).wait_send()
            for i in range(HOP_B):
                ctx_copy(h, ring(i) * 2 + c, 1, dev_b).wait_send()
            for zz in range(NZ):
                ctx_copy(h, zz * 2 + c, 2, dev_sib).wait_send()

    local[7].wait()
    for h in range(HEADS):
        hvbuf[c, :, h * 128 : (h + 1) * 128] = nn_dot(att[h], wuv[:, h * 128 : (h + 1) * 128]).astype(BF16)
    hv_copy = pltpu.make_async_remote_copy(
        src_ref=hvbuf.at[c], dst_ref=hvbuf.at[c], send_sem=hv_send, recv_sem=hv_recv,
        device_id=dev_sib, device_id_type=MESH,
    )
    hv_arrive = pltpu.make_async_remote_copy(
        src_ref=hvbuf.at[1 - c], dst_ref=hvbuf.at[1 - c], send_sem=hv_send, recv_sem=hv_recv,
        device_id=dev_sib, device_id_type=MESH,
    )
    hv_copy.start()
    local[8].wait()
    w_arrive.wait_recv()
    hv_arrive.wait_recv()

    def block_rows(zb):
        return pl.ds(pl.multiple_of((zb // 4) * BR, 16), BR)

    def partials(index, zb):
        cols = pl.ds(pl.multiple_of((zb % 4) * BC, 128), BC)
        both = nn_dot(hvbuf[0], wout[0, :, cols]) + nn_dot(hvbuf[1], wout[1, :, cols])
        part[index, 0] = both[0:BR]
        part[index, 1] = both[BR : 2 * BR]

    targets_of = (dev_a2, dev_a, dev_b, dev_a, dev_b, dev_a2, dev_b2)

    def push(i):
        return pltpu.make_async_remote_copy(
            src_ref=snd.at[i], dst_ref=rcv.at[i], send_sem=r_send.at[i], recv_sem=r_recv.at[i],
            device_id=targets_of[i], device_id_type=MESH,
        )

    def send(i, value):
        snd[i] = value.astype(BF16)
        push(i).start()

    def received(i):
        push(i).wait_recv()
        return rcv[i].astype(F32)

    far, side, back = ring(4), ring(3), ring(-3)
    near_a, near_b, mid_a, mid_b = ring(1), ring(-1), ring(2), ring(-2)
    partials(0, far)
    send(0, part[0, far // 4])
    partials(1, side)
    send(1, part[1, side // 4])
    partials(2, back)
    send(2, part[2, back // 4])
    partials(3, mid_a)
    for i in range(3):
        push(i).wait_send()
    send(3, part[2, near_a // 4])
    send(4, part[1, near_b // 4])
    send(5, part[3, mid_a // 4] + received(0) + received(1))
    send(6, part[3, mid_b // 4] + received(2))
    own = part[0, z // 4] + received(3) + received(4)
    own = own + received(6)
    own = own + received(5)

    def drain_reduce():
        hv_copy.wait_send()
        for i in range(3, 7):
            push(i).wait_send()

    ways = (dev_a, dev_a2, dev_b, dev_b2, dev_sib)

    def hid_copy(zb, way):
        return pltpu.make_async_remote_copy(
            src_ref=hid.at[c, zb], dst_ref=hid.at[c, zb], send_sem=h_send.at[zb, way],
            recv_sem=h_recv.at[c, zb], device_id=ways[way], device_id_type=MESH,
        )

    def hid_sibling(zb):
        return pltpu.make_async_remote_copy(
            src_ref=hid.at[1 - c, zb], dst_ref=hid.at[1 - c, zb], send_sem=h_send.at[zb, 4],
            recv_sem=h_recv.at[1 - c, zb], device_id=dev_sib, device_id_type=MESH,
        )

    lg[...] = jnp.zeros_like(lg)
    ss[...] = jnp.zeros_like(ss)

    def use(core, zb):
        rows = block_rows(zb)
        x = hid[core, zb]
        depth = pl.ds(pl.multiple_of(core * HALF + (zb % 4) * BC, 128), BC)
        lg[rows, :] += nn_dot(x, wvoc[depth, :])
        wide = x.astype(F32)
        square = wide * wide
        total = square[:, 0:128]
        for j in range(1, BC // 128):
            total = total + square[:, j * 128 : (j + 1) * 128]
        ss[rows, :] += total

    hid[c, z] = own.astype(BF16)
    for way in (1, 3, 4):
        hid_copy(z, way).start()
    hid_copy(z, 1).wait_send()
    hid_copy(z, 3).wait_send()
    hid_copy(z, 0).start()
    hid_copy(z, 2).start()
    local[9].wait()
    use(c, z)

    def take(zb, onward):
        hid_copy(zb, 0).wait_recv()
        for way in onward:
            hid_copy(zb, way).start()
        hid_copy(zb, 4).start()

    def use_sibling(zb):
        hid_sibling(zb).wait_recv()
        use(1 - c, zb)

    use_sibling(z)
    take(ring(-2), (1, 0))
    take(ring(2), (2,))
    use(c, ring(-2))
    use(c, ring(2))
    take(ring(-1), ())
    take(ring(1), ())
    use(c, ring(-1))
    use(c, ring(1))
    for step in (2, -2, 1, -1):
        use_sibling(ring(step))
    take(ring(-3), ())
    take(ring(3), ())
    use(c, ring(-3))
    use(c, ring(3))
    take(ring(4), ())
    use(c, ring(4))
    for step in (3, -3, 4):
        use_sibling(ring(step))

    def drain_hidden():
        hid_copy(z, 0).wait_send()
        hid_copy(z, 2).wait_send()
        hid_copy(ring(-2), 0).wait_send()
        hid_copy(ring(-2), 1).wait_send()
        hid_copy(ring(2), 2).wait_send()
        for zz in range(NZ):
            hid_copy(zz, 4).wait_send()

    local[10].wait()
    lane = lax.broadcasted_iota(jnp.int32, (ROWS, 128), 1)
    wide_targets = jnp.concatenate(
        [target_ref[...].astype(F32), jnp.zeros((REQ, 96), F32)], axis=1
    )
    wide_targets = jnp.concatenate([wide_targets, jnp.zeros((8 - REQ, 128), F32)], axis=0)
    turned = jnp.transpose(jnp.concatenate([wide_targets] * 16, axis=0))
    target_col = jnp.concatenate([turned[0:32, k : k + 1] for k in range(REQ)], axis=0).astype(jnp.int32)
    factor = lax.rsqrt(jnp.sum(ss[...], axis=1, keepdims=True) * (1.0 / D) + norm_epsilon)
    logits = lg[...] * factor
    top = jnp.max(logits, axis=1, keepdims=True)
    total = jnp.sum(jnp.exp(logits - top), axis=1, keepdims=True)
    hit = lax.broadcasted_iota(jnp.int32, (ROWS, VOCAB_LOCAL), 1) == target_col - t * VOCAB_LOCAL
    aimed = jnp.sum(jnp.where(hit, logits, 0.0), axis=1, keepdims=True)
    table = jnp.where(lane == 0, top, jnp.where(lane == 1, total, jnp.where(lane == 2, aimed, 0.0)))
    table = jnp.concatenate([table, jnp.zeros((128 - ROWS, 128), F32)], axis=0)
    stat[t] = jnp.transpose(table)[0:8, :]

    def stat_copy(d):
        return pltpu.make_async_remote_copy(
            src_ref=stat.at[t], dst_ref=stat.at[t], send_sem=st_send.at[d], recv_sem=st_recv.at[t],
            device_id={"tp": lax.rem(t + d, NT)}, device_id_type=MESH,
        )

    def stat_arrive(d):
        peer = lax.rem(t + d, NT)
        return pltpu.make_async_remote_copy(
            src_ref=stat.at[peer], dst_ref=stat.at[peer], send_sem=st_send.at[d], recv_sem=st_recv.at[peer],
            device_id={"tp": peer}, device_id_type=MESH,
        )

    for d in range(1, NT):
        stat_copy(d).start()

    local[11].wait()
    lane1 = lax.broadcasted_iota(jnp.int32, (1, 128), 1)
    lengths = jnp.concatenate([reply_len[...].astype(F32), jnp.zeros((REQ, 120), F32)], axis=1)
    lengths = jnp.concatenate([lengths, jnp.zeros((8 - REQ, 128), F32)], axis=0)
    sub8 = lax.broadcasted_iota(jnp.int32, (8, 128), 0)
    lane8 = lax.broadcasted_iota(jnp.int32, (8, 128), 1)
    sub128 = lax.broadcasted_iota(jnp.int32, (128, 128), 0)
    lane128 = lax.broadcasted_iota(jnp.int32, (128, 128), 1)
    to_lanes = ((lane128 % 32) // STEPS == sub128).astype(BF16)
    lengths = jnp.where(lane8 // 32 == sub8, nn_dot(lengths.astype(BF16), to_lanes), 0.0)
    lengths = jnp.sum(lengths, axis=0, keepdims=True)
    lengths = jnp.where(lane1 < ROWS, lengths, 1.0)

    drain_route()
    drain_ctx()
    drain_reduce()
    drain_hidden()
    for d in range(1, NT):
        stat_arrive(d).wait_recv()
    every = [stat[d] for d in range(NT)]
    joint = functools.reduce(jnp.maximum, [one[0:1] for one in every])
    joint_total = functools.reduce(jnp.add, [one[1:2] * jnp.exp(one[0:1] - joint) for one in every])
    joint_aimed = functools.reduce(jnp.add, [one[2:3] for one in every])
    log_prob = joint_aimed - (joint + jnp.log(joint_total))
    inside = jnp.logical_and((lane1 % STEPS).astype(F32) < lengths, lane1 < ROWS)
    value = jnp.where(inside, log_prob, 0.0) / lengths
    spread = jnp.where(lane8 // 32 == sub8, jnp.broadcast_to(value, (8, 128)), 0.0)
    pick = ((sub128 % 32) // STEPS == lane128).astype(F32)
    summed = lax.dot_general(
        spread, pick, (((1,), (0,)), ((), ())), precision=lax.Precision.HIGHEST, preferred_element_type=F32
    )
    score_ref[...] = summed[0:REQ, 0:CAND]
    for d in range(1, NT):
        stat_copy(d).wait_send()


def per_device(
    ctx_latent, ctx_rope, ctx_scale, dest, ctx_len, queries, reply_keys, reply_len, targets, w_uv, w_out, w_vocab
):
    vmem = pl.BlockSpec(memory_space=pltpu.VMEM)
    smem = pltpu.SMEM
    hbm = pl.BlockSpec(memory_space=pltpu.HBM)
    dma = pltpu.SemaphoreType.DMA
    return pl.pallas_call(
        kernel,
        out_shape=jax.ShapeDtypeStruct((REQ, CAND), F32),
        in_specs=[hbm] * 12,
        out_specs=vmem,
        scratch_shapes=[
            smem((48,), jnp.int32),
            smem((REQ,), jnp.int32),
            pltpu.VMEM((REQ, CAND), jnp.int32),
            pltpu.VMEM((REQ, 64, KVR), BF16),
            pltpu.VMEM((REQ, 32, 128), BF16),
            pltpu.VMEM((REQ, 4, 64), BF16),
            pltpu.VMEM((REQ, CAND, STEPS * KEY), BF16),
            pltpu.VMEM((REQ, 32), jnp.int32),
            pltpu.VMEM((REQ, 2, 16, WIDE_A), BF16),
            pltpu.VMEM((REQ, 2, 16, WIDE_B), BF16),
            pltpu.VMEM((2, NG, 2, 16, WIDE_A), BF16),
            pltpu.VMEM((2, NG, 2, 16, WIDE_B), BF16),
            pltpu.VMEM((NG * 2, 16, WIDE_A), BF16),
            pltpu.VMEM((NG * 2, 16, WIDE_B), BF16),
            pltpu.VMEM((NG * 2, 16, WIDE_A), BF16),
            pltpu.VMEM((NG * 2, 16, WIDE_B), BF16),
            pltpu.VMEM((2, NT, REQ, 16, WIDE_A), BF16),
            pltpu.VMEM((2, NT, REQ, 16, WIDE_B), BF16),
            pltpu.VMEM((REQ, 32, HEADS * KEY), BF16),
            pltpu.VMEM((REQ, QROWS, KVR), BF16),
            pltpu.VMEM((REQ, 2 * QROWS, 128), BF16),
            pltpu.VMEM((32, KVR), BF16),
            pltpu.VMEM((32, 128), BF16),
            pltpu.VMEM((REQ, QROWS, 1), F32),
            pltpu.VMEM((REQ, QROWS, 1), F32),
            pltpu.VMEM((REQ, QROWS, KVR), F32),
            pltpu.VMEM((HEADS, ROWS, KVR), BF16),
            pltpu.VMEM((2, ROWS, 512), BF16),
            pltpu.VMEM((KVR, 512), BF16),
            pltpu.VMEM((2, 512, HALF), BF16),
            pltpu.VMEM((D, VOCAB_LOCAL), BF16),
            pltpu.VMEM((4, 2, BR, BC), F32),
            pltpu.VMEM((7, BR, BC), BF16),
            pltpu.VMEM((7, BR, BC), BF16),
            pltpu.VMEM((2, NZ, BR, BC), BF16),
            pltpu.VMEM((ROWS, VOCAB_LOCAL), F32),
            pltpu.VMEM((ROWS, 128), F32),
            pltpu.VMEM((NT, 8, 128), F32),
            dma((12,)),
            dma((CHUNKS, NG)),
            dma((CHUNKS, NG)),
            dma((CHUNKS, NT, 3)),
            dma((CHUNKS, NT)),
            dma, dma, dma, dma,
            dma((7,)), dma((7,)),
            dma((NZ, 5)), dma((2, NZ)),
            dma((NT,)), dma((NT,)),
        ],
        compiler_params=pltpu.CompilerParams(
            collective_id=0, has_side_effects=True, vmem_limit_bytes=62 * 1024 * 1024
        ),
    )(
        dest, ctx_len, reply_len, ctx_latent, ctx_rope, jnp.swapaxes(ctx_scale, 1, 2), reply_keys, targets,
        queries, w_uv, w_out, w_vocab,
    )


def solution(mesh):
    group = ("section", "grp")
    placed = (
        P(group, "tp", None),
        P(group, "tp", None),
        P(group, "tp", None),
        P(),
        P(group),
        P(group, None, "tp"),
        P(group, None, None),
        P(group, None),
        P(group, None),
        P(None, "tp"),
        P("tp", None),
        P(None, "tp"),
    )
    return jax.shard_map(
        per_device, mesh=mesh, in_specs=placed, out_specs=P(group, None), check_vma=False
    )
```

```python
import functools

import jax
import jax.numpy as jnp
from jax import lax
from jax.experimental import pallas as pl
from jax.experimental.pallas import tpu as pltpu
from jax.sharding import PartitionSpec as P

MESH = pl.DeviceIdType.MESH
BF16, F32 = jnp.bfloat16, jnp.float32

softmax_scale = 192.0 ** (-0.5)
norm_epsilon = 1e-06

NS, NG, NZ, NT = 4, 4, 8, 16
REQ, CAND, STEPS, HEADS = 3, 8, 4, 4
KVR, ROPE, KEY = 512, 64, 576
ROWS = REQ * CAND * STEPS
QROWS = HEADS * CAND * STEPS
D, HALF = 7168, 3584
BR, BC = 48, 896
HOP_A, HOP_B = 4, 3
WIDE_A, WIDE_B = 640, 512
CHUNKS = 4
VOCAB_LOCAL = 256
ROUTE, USE = -1, -2
SCHEDULE = (
    (1, ROUTE), (0, 0), (2, ROUTE), (1, 0), (0, 1), (3, ROUTE), (2, 0), (1, 1), (0, 2), (3, 0), (2, 1), (1, 2), (0, 3),
    (3, 1), (2, 2), (1, 3), (0, 4), (3, 2), (2, 3), (1, 4), (0, USE), (3, 3), (2, 4), (1, USE), (2, USE), (3, 4), (3, USE),
)


def nt_dot(a, b):
    return lax.dot_general(a, b, (((1,), (1,)), ((), ())), preferred_element_type=F32)


def nn_dot(a, b):
    return lax.dot_general(a, b, (((1,), (0,)), ((), ())), preferred_element_type=F32)


def unpack_key(slab, index):
    n = slab.shape[0]
    low = lax.broadcasted_iota(jnp.int32, (n, 128), 1) < ROPE
    start = index * KEY
    first = start // 128
    if index % 2 == 0:
        latent = slab[:, start : start + KVR]
        tile = slab[:, start + KVR : start + KVR + 128]
        rope_low = jnp.where(low, tile, 0.0)
        rope_high = pltpu.roll(rope_low, 64, 1)
    else:
        turned = [
            pltpu.roll(slab[:, (first + j) * 128 : (first + j + 1) * 128], 64, 1) for j in range(5)
        ]
        latent = jnp.concatenate([jnp.where(low, turned[j], turned[j + 1]) for j in range(4)], axis=1)
        rope_low = jnp.where(low, turned[4], 0.0)
        rope_high = pltpu.roll(rope_low, 64, 1)
    return latent, rope_low, rope_high


def kernel(
    dest_hbm, ctx_len_hbm, reply_len_hbm, lat_hbm, rope_hbm, scale_hbm, reply_hbm, target_hbm,
    query_hbm, uv_hbm, out_hbm, vocab_hbm,
    score_ref,
    dest, ctx_len, reply_len, lat_ref, rope_ref, scale_ref, reply_ref, target_ref, xsrc_a, xsrc_b, sbuf_a, sbuf_b, rbuf_0, rbuf_1, rbuf_2, rbuf_3, ctx_a, ctx_b, q_in, qn, qr, rkn, rkr, m_s, l_s, acc_s, att, hvbuf, wuv, wout, wvoc,
    part, snd, rcv, hid, lg, ss, stat,
    local_sem, route_send, route_recv, ctx_send, ctx_recv, w_send, w_recv, hv_send, hv_recv,
    r_send, r_recv, h_send, h_recv, st_send, st_recv,
):
    s, g, t = lax.axis_index("section"), lax.axis_index("grp"), lax.axis_index("tp")
    z, c = t // 2, t % 2
    sib = t + 1 - 2 * c
    sgn = 1 - 2 * c
    xsrc, sbuf, ctx = (xsrc_a, xsrc_b), (sbuf_a, sbuf_b), (ctx_a, ctx_b)
    rbuf = (rbuf_0, rbuf_1, rbuf_2, rbuf_3)
    next_s = lax.rem(s + 1, NS)
    prev_s = lax.rem(s + NS - 1, NS)

    def ring(step):
        return lax.rem(z + sgn * step + 2 * NZ, NZ)

    dev_a, dev_b = {"tp": ring(1) * 2 + c}, {"tp": ring(-1) * 2 + c}
    dev_a2, dev_b2 = {"tp": ring(2) * 2 + c}, {"tp": ring(-2) * 2 + c}
    dev_sib = {"tp": sib}

    barrier = pltpu.get_barrier_semaphore()
    for k in range(NG):
        pl.semaphore_signal(barrier, inc=1, device_id={"section": prev_s, "grp": k}, device_id_type=MESH)
    for device in (dev_a, dev_b, dev_a2, dev_b2, dev_sib):
        pl.semaphore_signal(barrier, inc=1, device_id=device, device_id_type=MESH)

    own_cols = pl.ds(pl.multiple_of(c * HALF, 128), HALF)
    other_cols = pl.ds(pl.multiple_of((1 - c) * HALF, 128), HALF)
    pairs = [
        (scale_hbm, scale_ref), (lat_hbm, lat_ref), (rope_hbm, rope_ref), (dest_hbm, dest),
        (query_hbm, q_in), (reply_hbm, reply_ref), (ctx_len_hbm, ctx_len),
        (uv_hbm, wuv), (out_hbm.at[:, own_cols], wout.at[c]), (vocab_hbm, wvoc),
        (target_hbm, target_ref), (reply_len_hbm, reply_len),
    ]
    local = [pltpu.make_async_copy(a, b, local_sem.at[i]) for i, (a, b) in enumerate(pairs)]
    for copy in local:
        copy.start()

    row = lax.broadcasted_iota(jnp.int32, (64, 64), 0)
    col = lax.broadcasted_iota(jnp.int32, (64, 64), 1)
    place = 2 * ((row // 32) * 16 + row % 16) + (row // 16) % 2
    perm = (col == place).astype(BF16)
    for copy in local[:4]:
        copy.wait()
    scales = jnp.concatenate([scale_ref[j].astype(F32) for j in range(REQ)] + [jnp.zeros((4, 64), F32)], axis=0)
    scales = jnp.concatenate([scales, jnp.zeros((16, 64), F32)], axis=1)
    scales = jnp.transpose(jnp.concatenate([scales] * 8, axis=0))
    for j in range(REQ):
        parts = [
            (lat_ref[j, :, b * 128 : (b + 1) * 128].astype(F32) * scales[0:64, j * 4 + b : j * 4 + b + 1]).astype(BF16)
            for b in range(4)
        ]
        moved = nn_dot(perm, jnp.concatenate(parts, axis=1)).astype(BF16)
        for h in range(2):
            xsrc_a[j, h, :, 0:KVR] = moved[h * 32 : h * 32 + 16]
            xsrc_a[j, h, :, KVR:WIDE_A] = rope_ref[j, h * 16 : (h + 1) * 16, :]
            xsrc_b[j, h] = moved[h * 32 + 16 : h * 32 + 32]

    own_dest = [dest[(s * NG + g) * REQ + j] for j in range(REQ)]
    for h in range(CHUNKS):
        for k in range(NG):
            first = jnp.where(own_dest[0] == k, 0, jnp.where(own_dest[1] == k, 1, 2))
            last = jnp.where(own_dest[2] == k, 2, jnp.where(own_dest[1] == k, 1, 0))
            sbuf[h % 2][h // 2, k, 0] = xsrc[h % 2][first, h // 2]
            sbuf[h % 2][h // 2, k, 1] = xsrc[h % 2][last, h // 2]

    pl.semaphore_wait(barrier, NG + 5)

    def route(h, j):
        k = lax.rem(g + j, NG)
        return pltpu.make_async_remote_copy(
            src_ref=sbuf[h % 2].at[h // 2, k], dst_ref=rbuf[h].at[pl.ds(2 * g, 2)],
            send_sem=route_send.at[h, j], recv_sem=route_recv.at[h, g],
            device_id={"section": next_s, "grp": k}, device_id_type=MESH,
        )

    def route_arrived(h, k):
        return pltpu.make_async_remote_copy(
            src_ref=sbuf[h % 2].at[h // 2, k], dst_ref=rbuf[h].at[pl.ds(2 * k, 2)],
            send_sem=route_send.at[h, k], recv_sem=route_recv.at[h, k],
            device_id={"section": next_s, "grp": k}, device_id_type=MESH,
        )

    def route_start(h):
        for k in range(NG):
            route(h, k).start()

    def route_left(h):
        for k in range(NG):
            route(h, k).wait_send()

    route_start(0)
    w_copy = pltpu.make_async_remote_copy(
        src_ref=out_hbm.at[:, other_cols], dst_ref=wout.at[c],
        send_sem=w_send, recv_sem=w_recv, device_id=dev_sib, device_id_type=MESH,
    )
    w_arrive = pltpu.make_async_remote_copy(
        src_ref=out_hbm.at[:, other_cols], dst_ref=wout.at[1 - c],
        send_sem=w_send, recv_sem=w_recv, device_id=dev_sib, device_id_type=MESH,
    )

    def drain_route():
        route_left(CHUNKS - 1)
        w_copy.wait_send()

    picks = [jnp.int32(0)] * REQ
    count = jnp.int32(0)
    for h in range(NG):
        seen = jnp.int32(0)
        for j in range(REQ):
            hit = dest[(prev_s * NG + h) * REQ + j] == g
            for k in range(REQ):
                picks[k] = jnp.where(jnp.logical_and(hit, count == k), h * 2 + seen, picks[k])
            one = jnp.where(hit, 1, 0)
            seen = seen + one
            count = count + one
    picks = [jnp.minimum(pick, 2 * NG - 1) for pick in picks]

    for copy in local[4:7]:
        copy.wait()
    a_row = (lax.broadcasted_iota(jnp.int32, (QROWS, 32), 0) % 32) // STEPS
    t_row = lax.broadcasted_iota(jnp.int32, (QROWS, 32), 0) % STEPS
    a_col = lax.broadcasted_iota(jnp.int32, (QROWS, 32), 1) % CAND
    u_col = lax.broadcasted_iota(jnp.int32, (QROWS, 32), 1) // CAND
    reply_seen = jnp.logical_and(a_row == a_col, u_col <= t_row)

    def prepare(k, carry):
        slab = q_in[k].astype(F32)
        for h in range(HEADS):
            latent, low, high = unpack_key(slab, h)
            qn[k, h * 32 : (h + 1) * 32, :] = latent.astype(BF16)
            qr[k, h * 32 : (h + 1) * 32, :] = low.astype(BF16)
            qr[k, QROWS + h * 32 : QROWS + (h + 1) * 32, :] = high.astype(BF16)
        keys = reply_ref[k].astype(F32)
        pieces = [unpack_key(keys, u) for u in range(STEPS)]
        rkn[...] = jnp.concatenate([piece[0] for piece in pieces], axis=0).astype(BF16)
        rkr[...] = jnp.concatenate([piece[1] for piece in pieces], axis=0).astype(BF16)
        scores = nt_dot(qn[k], rkn[...]) + nt_dot(qr[k, 0:QROWS], rkr[...])
        scores = jnp.where(reply_seen, scores * softmax_scale, -jnp.inf)
        top = jnp.max(scores, axis=1, keepdims=True)
        weight = jnp.exp(scores - top)
        m_s[k] = top
        l_s[k] = jnp.sum(weight, axis=1, keepdims=True)
        acc_s[k] = nn_dot(weight.astype(BF16), rkn[...])
        return carry

    lax.fori_loop(0, REQ, prepare, 0)

    def ctx_copy(h, slot, way, device):
        block = ctx[h % 2].at[h // 2, slot]
        return pltpu.make_async_remote_copy(
            src_ref=block, dst_ref=block, send_sem=ctx_send.at[h, slot, way], recv_sem=ctx_recv.at[h, slot],
            device_id=device, device_id_type=MESH,
        )

    ctx_ways = (dev_a, dev_b, dev_sib)

    def open_chunk(h):
        for k in range(NG):
            route_arrived(h, k).wait_recv()
        for k in range(REQ):
            ctx[h % 2][h // 2, t, k] = rbuf[h][picks[k]]
        for way in range(3):
            ctx_copy(h, t, way, ctx_ways[way]).start()

    def share(h, slot, *onward):
        ctx_copy(h, slot, 0, dev_a).wait_recv()
        for way in onward:
            ctx_copy(h, slot, way, ctx_ways[way]).start()
        ctx_copy(h, slot, 2, dev_sib).start()

    def hop(h, i):
        share(h, ring(-i) * 2 + c, *((0,) if i < HOP_A else ()))
        if i <= HOP_B:
            share(h, ring(i) * 2 + c, *((1,) if i < HOP_B else ()))

    n_col = lax.broadcasted_iota(jnp.int32, (QROWS, 256), 1)
    n_pos = (n_col // 16) * 64 + 2 * (n_col % 16)

    def attend(h):
        latent, scores = [], []
        for k in range(REQ):
            if h % 2 == 0:
                latent.append(ctx_a[h // 2, :, k, :, 0:KVR].reshape(256, KVR))
            else:
                latent.append(ctx_b[h // 2, :, k].reshape(256, KVR))
            rope = ctx_a[h // 2, :, k, :, KVR:WIDE_A].reshape(256, 128)
            rope_query = qr[k, (h % 2) * QROWS : (h % 2 + 1) * QROWS]
            one = (nt_dot(qn[k], latent[k]) + nt_dot(rope_query, rope)) * softmax_scale
            scores.append(jnp.where(n_pos + (h // 2) * 32 + h % 2 < ctx_len[k], one, -jnp.inf))
        old = [m_s[k] for k in range(REQ)]
        top = [jnp.maximum(old[k], jnp.max(scores[k], axis=1, keepdims=True)) for k in range(REQ)]
        weight = [jnp.exp(scores[k] - top[k]) for k in range(REQ)]
        fade = [jnp.exp(old[k] - top[k]) for k in range(REQ)]
        value = [nn_dot(weight[k].astype(BF16), latent[k]) for k in range(REQ)]
        total = [l_s[k] * fade[k] + jnp.sum(weight[k], axis=1, keepdims=True) for k in range(REQ)]
        for k in range(REQ):
            m_s[k] = top[k]
            l_s[k] = total[k]
            acc_s[k] = acc_s[k] * fade[k] + value[k]

    def close_chunk(h):
        def one(zz, carry):
            ctx_copy(h, zz * 2 + 1 - c, 2, dev_sib).wait_recv()
            return carry

        lax.fori_loop(0, NZ, one, 0)

    for h, i in SCHEDULE:
        if i == ROUTE:
            route_left(h - 1)
            route_start(h)
            if h == CHUNKS - 1:
                w_copy.start()
        elif i == USE:
            close_chunk(h)
            attend(h)
        elif i == 0:
            open_chunk(h)
        else:
            hop(h, i)
    for k in range(REQ):
        rows = (acc_s[k] / l_s[k]).astype(BF16)
        for h in range(HEADS):
            att[h, k * 32 : (k + 1) * 32, :] = rows[h * 32 : (h + 1) * 32]

    def drain_ctx():
        for h in range(CHUNKS):
            for i in range(HOP_A):
                ctx_copy(h, ring(-i) * 2 + c, 0, dev_a).wait_send()
            for i in range(HOP_B):
                ctx_copy(h, ring(i) * 2 + c, 1, dev_b).wait_send()
            for zz in range(NZ):
                ctx_copy(h, zz * 2 + c, 2, dev_sib).wait_send()

    local[7].wait()
    for h in range(HEADS):
        hvbuf[c, :, h * 128 : (h + 1) * 128] = nn_dot(att[h], wuv[:, h * 128 : (h + 1) * 128]).astype(BF16)
    hv_copy = pltpu.make_async_remote_copy(
        src_ref=hvbuf.at[c], dst_ref=hvbuf.at[c], send_sem=hv_send, recv_sem=hv_recv,
        device_id=dev_sib, device_id_type=MESH,
    )
    hv_arrive = pltpu.make_async_remote_copy(
        src_ref=hvbuf.at[1 - c], dst_ref=hvbuf.at[1 - c], send_sem=hv_send, recv_sem=hv_recv,
        device_id=dev_sib, device_id_type=MESH,
    )
    hv_copy.start()
    local[8].wait()
    w_arrive.wait_recv()
    hv_arrive.wait_recv()

    def block_rows(zb):
        return pl.ds(pl.multiple_of((zb // 4) * BR, 16), BR)

    def partials(index, zb):
        cols = pl.ds(pl.multiple_of((zb % 4) * BC, 128), BC)
        both = nn_dot(hvbuf[0], wout[0, :, cols]) + nn_dot(hvbuf[1], wout[1, :, cols])
        part[index, 0] = both[0:BR]
        part[index, 1] = both[BR : 2 * BR]

    targets_of = (dev_a2, dev_a, dev_b, dev_a, dev_b, dev_a2, dev_b2)

    def push(i):
        return pltpu.make_async_remote_copy(
            src_ref=snd.at[i], dst_ref=rcv.at[i], send_sem=r_send.at[i], recv_sem=r_recv.at[i],
            device_id=targets_of[i], device_id_type=MESH,
        )

    def send(i, value):
        snd[i] = value.astype(BF16)
        push(i).start()

    def received(i):
        push(i).wait_recv()
        return rcv[i].astype(F32)

    far, side, back = ring(4), ring(3), ring(-3)
    near_a, near_b, mid_a, mid_b = ring(1), ring(-1), ring(2), ring(-2)
    partials(0, far)
    send(0, part[0, far // 4])
    partials(1, side)
    send(1, part[1, side // 4])
    partials(2, back)
    send(2, part[2, back // 4])
    partials(3, mid_a)
    for i in range(3):
        push(i).wait_send()
    send(3, part[2, near_a // 4])
    send(4, part[1, near_b // 4])
    send(5, part[3, mid_a // 4] + received(0) + received(1))
    send(6, part[3, mid_b // 4] + received(2))
    own = part[0, z // 4] + received(3) + received(4)
    own = own + received(6)
    own = own + received(5)

    def drain_reduce():
        hv_copy.wait_send()
        for i in range(3, 7):
            push(i).wait_send()

    ways = (dev_a, dev_a2, dev_b, dev_b2, dev_sib)

    def hid_copy(zb, way):
        return pltpu.make_async_remote_copy(
            src_ref=hid.at[c, zb], dst_ref=hid.at[c, zb], send_sem=h_send.at[zb, way],
            recv_sem=h_recv.at[c, zb], device_id=ways[way], device_id_type=MESH,
        )

    def hid_sibling(zb):
        return pltpu.make_async_remote_copy(
            src_ref=hid.at[1 - c, zb], dst_ref=hid.at[1 - c, zb], send_sem=h_send.at[zb, 4],
            recv_sem=h_recv.at[1 - c, zb], device_id=dev_sib, device_id_type=MESH,
        )

    lg[...] = jnp.zeros_like(lg)
    ss[...] = jnp.zeros_like(ss)

    def use(core, zb):
        rows = block_rows(zb)
        x = hid[core, zb]
        depth = pl.ds(pl.multiple_of(core * HALF + (zb % 4) * BC, 128), BC)
        lg[rows, :] += nn_dot(x, wvoc[depth, :])
        wide = x.astype(F32)
        square = wide * wide
        total = square[:, 0:128]
        for j in range(1, BC // 128):
            total = total + square[:, j * 128 : (j + 1) * 128]
        ss[rows, :] += total

    hid[c, z] = own.astype(BF16)
    for way in (1, 3, 4):
        hid_copy(z, way).start()
    hid_copy(z, 1).wait_send()
    hid_copy(z, 3).wait_send()
    hid_copy(z, 0).start()
    hid_copy(z, 2).start()
    local[9].wait()
    use(c, z)

    def take(zb, onward):
        hid_copy(zb, 0).wait_recv()
        for way in onward:
            hid_copy(zb, way).start()
        hid_copy(zb, 4).start()

    def use_sibling(zb):
        hid_sibling(zb).wait_recv()
        use(1 - c, zb)

    use_sibling(z)
    take(ring(-2), (1, 0))
    take(ring(2), (2,))
    use(c, ring(-2))
    use(c, ring(2))
    take(ring(-1), ())
    take(ring(1), ())
    use(c, ring(-1))
    use(c, ring(1))
    for step in (2, -2, 1, -1):
        use_sibling(ring(step))
    take(ring(-3), ())
    take(ring(3), ())
    use(c, ring(-3))
    use(c, ring(3))
    take(ring(4), ())
    use(c, ring(4))
    for step in (3, -3, 4):
        use_sibling(ring(step))

    def drain_hidden():
        hid_copy(z, 0).wait_send()
        hid_copy(z, 2).wait_send()
        hid_copy(ring(-2), 0).wait_send()
        hid_copy(ring(-2), 1).wait_send()
        hid_copy(ring(2), 2).wait_send()
        for zz in range(NZ):
            hid_copy(zz, 4).wait_send()

    local[10].wait()
    lane = lax.broadcasted_iota(jnp.int32, (ROWS, 128), 1)
    wide_targets = jnp.concatenate(
        [target_ref[...].astype(F32), jnp.zeros((REQ, 96), F32)], axis=1
    )
    wide_targets = jnp.concatenate([wide_targets, jnp.zeros((8 - REQ, 128), F32)], axis=0)
    turned = jnp.transpose(jnp.concatenate([wide_targets] * 16, axis=0))
    target_col = jnp.concatenate([turned[0:32, k : k + 1] for k in range(REQ)], axis=0).astype(jnp.int32)
    factor = lax.rsqrt(jnp.sum(ss[...], axis=1, keepdims=True) * (1.0 / D) + norm_epsilon)
    logits = lg[...] * factor
    top = jnp.max(logits, axis=1, keepdims=True)
    total = jnp.sum(jnp.exp(logits - top), axis=1, keepdims=True)
    hit = lax.broadcasted_iota(jnp.int32, (ROWS, VOCAB_LOCAL), 1) == target_col - t * VOCAB_LOCAL
    aimed = jnp.sum(jnp.where(hit, logits, 0.0), axis=1, keepdims=True)
    table = jnp.where(lane == 0, top, jnp.where(lane == 1, total, jnp.where(lane == 2, aimed, 0.0)))
    table = jnp.concatenate([table, jnp.zeros((128 - ROWS, 128), F32)], axis=0)
    stat[t] = jnp.transpose(table)[0:8, :]

    def stat_copy(d):
        return pltpu.make_async_remote_copy(
            src_ref=stat.at[t], dst_ref=stat.at[t], send_sem=st_send.at[d], recv_sem=st_recv.at[t],
            device_id={"tp": lax.rem(t + d, NT)}, device_id_type=MESH,
        )

    def stat_arrive(d):
        peer = lax.rem(t + d, NT)
        return pltpu.make_async_remote_copy(
            src_ref=stat.at[peer], dst_ref=stat.at[peer], send_sem=st_send.at[d], recv_sem=st_recv.at[peer],
            device_id={"tp": peer}, device_id_type=MESH,
        )

    for d in range(1, NT):
        stat_copy(d).start()

    local[11].wait()
    lane1 = lax.broadcasted_iota(jnp.int32, (1, 128), 1)
    lengths = jnp.concatenate([reply_len[...].astype(F32), jnp.zeros((REQ, 120), F32)], axis=1)
    lengths = jnp.concatenate([lengths, jnp.zeros((8 - REQ, 128), F32)], axis=0)
    sub8 = lax.broadcasted_iota(jnp.int32, (8, 128), 0)
    lane8 = lax.broadcasted_iota(jnp.int32, (8, 128), 1)
    sub128 = lax.broadcasted_iota(jnp.int32, (128, 128), 0)
    lane128 = lax.broadcasted_iota(jnp.int32, (128, 128), 1)
    to_lanes = ((lane128 % 32) // STEPS == sub128).astype(BF16)
    lengths = jnp.where(lane8 // 32 == sub8, nn_dot(lengths.astype(BF16), to_lanes), 0.0)
    lengths = jnp.sum(lengths, axis=0, keepdims=True)
    lengths = jnp.where(lane1 < ROWS, lengths, 1.0)

    drain_route()
    drain_ctx()
    drain_reduce()
    drain_hidden()
    for d in range(1, NT):
        stat_arrive(d).wait_recv()
    every = [stat[d] for d in range(NT)]
    joint = functools.reduce(jnp.maximum, [one[0:1] for one in every])
    joint_total = functools.reduce(jnp.add, [one[1:2] * jnp.exp(one[0:1] - joint) for one in every])
    joint_aimed = functools.reduce(jnp.add, [one[2:3] for one in every])
    log_prob = joint_aimed - (joint + jnp.log(joint_total))
    inside = jnp.logical_and((lane1 % STEPS).astype(F32) < lengths, lane1 < ROWS)
    value = jnp.where(inside, log_prob, 0.0) / lengths
    spread = jnp.where(lane8 // 32 == sub8, jnp.broadcast_to(value, (8, 128)), 0.0)
    pick = ((sub128 % 32) // STEPS == lane128).astype(F32)
    summed = lax.dot_general(
        spread, pick, (((1,), (0,)), ((), ())), precision=lax.Precision.HIGHEST, preferred_element_type=F32
    )
    score_ref[...] = summed[0:REQ, 0:CAND]
    for d in range(1, NT):
        stat_copy(d).wait_send()


def per_device(
    ctx_latent, ctx_rope, ctx_scale, dest, ctx_len, queries, reply_keys, reply_len, targets, w_uv, w_out, w_vocab
):
    vmem = pl.BlockSpec(memory_space=pltpu.VMEM)
    smem = pltpu.SMEM
    hbm = pl.BlockSpec(memory_space=pltpu.HBM)
    dma = pltpu.SemaphoreType.DMA
    return pl.pallas_call(
        kernel,
        out_shape=jax.ShapeDtypeStruct((REQ, CAND), F32),
        in_specs=[hbm] * 12,
        out_specs=vmem,
        scratch_shapes=[
            smem((48,), jnp.int32),
            smem((REQ,), jnp.int32),
            pltpu.VMEM((REQ, CAND), jnp.int32),
            pltpu.VMEM((REQ, 64, KVR), BF16),
            pltpu.VMEM((REQ, 32, 128), BF16),
            pltpu.VMEM((REQ, 4, 64), BF16),
            pltpu.VMEM((REQ, CAND, STEPS * KEY), BF16),
            pltpu.VMEM((REQ, 32), jnp.int32),
            pltpu.VMEM((REQ, 2, 16, WIDE_A), BF16),
            pltpu.VMEM((REQ, 2, 16, WIDE_B), BF16),
            pltpu.VMEM((2, NG, 2, 16, WIDE_A), BF16),
            pltpu.VMEM((2, NG, 2, 16, WIDE_B), BF16),
            pltpu.VMEM((NG * 2, 16, WIDE_A), BF16),
            pltpu.VMEM((NG * 2, 16, WIDE_B), BF16),
            pltpu.VMEM((NG * 2, 16, WIDE_A), BF16),
            pltpu.VMEM((NG * 2, 16, WIDE_B), BF16),
            pltpu.VMEM((2, NT, REQ, 16, WIDE_A), BF16),
            pltpu.VMEM((2, NT, REQ, 16, WIDE_B), BF16),
            pltpu.VMEM((REQ, 32, HEADS * KEY), BF16),
            pltpu.VMEM((REQ, QROWS, KVR), BF16),
            pltpu.VMEM((REQ, 2 * QROWS, 128), BF16),
            pltpu.VMEM((32, KVR), BF16),
            pltpu.VMEM((32, 128), BF16),
            pltpu.VMEM((REQ, QROWS, 1), F32),
            pltpu.VMEM((REQ, QROWS, 1), F32),
            pltpu.VMEM((REQ, QROWS, KVR), F32),
            pltpu.VMEM((HEADS, ROWS, KVR), BF16),
            pltpu.VMEM((2, ROWS, 512), BF16),
            pltpu.VMEM((KVR, 512), BF16),
            pltpu.VMEM((2, 512, HALF), BF16),
            pltpu.VMEM((D, VOCAB_LOCAL), BF16),
            pltpu.VMEM((4, 2, BR, BC), F32),
            pltpu.VMEM((7, BR, BC), BF16),
            pltpu.VMEM((7, BR, BC), BF16),
            pltpu.VMEM((2, NZ, BR, BC), BF16),
            pltpu.VMEM((ROWS, VOCAB_LOCAL), F32),
            pltpu.VMEM((ROWS, 128), F32),
            pltpu.VMEM((NT, 8, 128), F32),
            dma((12,)),
            dma((CHUNKS, NG)),
            dma((CHUNKS, NG)),
            dma((CHUNKS, NT, 3)),
            dma((CHUNKS, NT)),
            dma, dma, dma, dma,
            dma((7,)), dma((7,)),
            dma((NZ, 5)), dma((2, NZ)),
            dma((NT,)), dma((NT,)),
        ],
        compiler_params=pltpu.CompilerParams(
            collective_id=0, has_side_effects=True, vmem_limit_bytes=62 * 1024 * 1024
        ),
    )(
        dest, ctx_len, reply_len, ctx_latent, ctx_rope, jnp.swapaxes(ctx_scale, 1, 2), reply_keys, targets,
        queries, w_uv, w_out, w_vocab,
    )


def solution(mesh):
    group = ("section", "grp")
    placed = (
        P(group, "tp", None),
        P(group, "tp", None),
        P(group, "tp", None),
        P(),
        P(group),
        P(group, None, "tp"),
        P(group, None, None),
        P(group, None),
        P(group, None),
        P(None, "tp"),
        P("tp", None),
        P(None, "tp"),
    )
    return jax.shard_map(
        per_device, mesh=mesh, in_specs=placed, out_specs=P(group, None), check_vma=False
    )
```

```python
import functools

import jax
import jax.numpy as jnp
from jax import lax
from jax.experimental import pallas as pl
from jax.experimental.pallas import tpu as pltpu
from jax.sharding import PartitionSpec as P

MESH = pl.DeviceIdType.MESH
BF16, F32 = jnp.bfloat16, jnp.float32

softmax_scale = 192.0 ** (-0.5)
norm_epsilon = 1e-06

NS, NG, NZ, NT = 4, 4, 8, 16
REQ, CAND, STEPS, HEADS = 3, 8, 4, 4
KVR, ROPE, KEY = 512, 64, 576
ROWS = REQ * CAND * STEPS
QROWS = HEADS * CAND * STEPS
D, HALF = 7168, 3584
BR, BC = 48, 896
HOP_A, HOP_B = 4, 3
WIDE_A, WIDE_B = 640, 512
CHUNKS = 4
VOCAB_LOCAL = 256
ROUTE, USE = -1, -2
SCHEDULE = (
    (1, ROUTE), (0, 0), (2, ROUTE), (1, 0), (0, 1), (3, ROUTE), (2, 0), (1, 1), (0, 2), (3, 0), (2, 1), (1, 2), (0, 3),
    (3, 1), (2, 2), (1, 3), (0, 4), (3, 2), (2, 3), (1, 4), (0, USE), (3, 3), (2, 4), (1, USE), (2, USE), (3, 4), (3, USE),
)


def nt_dot(a, b):
    return lax.dot_general(a, b, (((1,), (1,)), ((), ())), preferred_element_type=F32)


def nn_dot(a, b):
    return lax.dot_general(a, b, (((1,), (0,)), ((), ())), preferred_element_type=F32)


def unpack_key(slab, index):
    n = slab.shape[0]
    low = lax.broadcasted_iota(jnp.int32, (n, 128), 1) < ROPE
    start = index * KEY
    first = start // 128
    if index % 2 == 0:
        latent = slab[:, start : start + KVR]
        tile = slab[:, start + KVR : start + KVR + 128]
        rope_low = jnp.where(low, tile, 0.0)
        rope_high = pltpu.roll(rope_low, 64, 1)
    else:
        turned = [
            pltpu.roll(slab[:, (first + j) * 128 : (first + j + 1) * 128], 64, 1) for j in range(5)
        ]
        latent = jnp.concatenate([jnp.where(low, turned[j], turned[j + 1]) for j in range(4)], axis=1)
        rope_low = jnp.where(low, turned[4], 0.0)
        rope_high = pltpu.roll(rope_low, 64, 1)
    return latent, rope_low, rope_high


def kernel(
    dest_hbm, ctx_len_hbm, reply_len_hbm, lat_hbm, rope_hbm, scale_hbm, reply_hbm, target_hbm,
    query_hbm, uv_hbm, out_hbm, vocab_hbm,
    score_ref,
    dest, ctx_len, reply_len, lat_ref, rope_ref, scale_ref, reply_ref, target_ref, xsrc_a, xsrc_b, sbuf_a, sbuf_b, rbuf_0, rbuf_1, rbuf_2, rbuf_3, ctx_a, ctx_b, q_in, qn, qr, rkn, rkr, m_s, l_s, acc_s, att, hvbuf, wuv, wout, wvoc,
    part, snd, rcv, hid, lg, ss, stat,
    local_sem, route_send, route_recv, ctx_send, ctx_recv, w_send, w_recv, hv_send, hv_recv,
    r_send, r_recv, h_send, h_recv, st_send, st_recv,
):
    s, g, t = lax.axis_index("section"), lax.axis_index("grp"), lax.axis_index("tp")
    z, c = t // 2, t % 2
    sib = t + 1 - 2 * c
    sgn = 1 - 2 * c
    xsrc, sbuf, ctx = (xsrc_a, xsrc_b), (sbuf_a, sbuf_b), (ctx_a, ctx_b)
    rbuf = (rbuf_0, rbuf_1, rbuf_2, rbuf_3)
    next_s = lax.rem(s + 1, NS)
    prev_s = lax.rem(s + NS - 1, NS)

    def ring(step):
        return lax.rem(z + sgn * step + 2 * NZ, NZ)

    dev_a, dev_b = {"tp": ring(1) * 2 + c}, {"tp": ring(-1) * 2 + c}
    dev_a2, dev_b2 = {"tp": ring(2) * 2 + c}, {"tp": ring(-2) * 2 + c}
    dev_sib = {"tp": sib}

    barrier = pltpu.get_barrier_semaphore()
    for k in range(NG):
        pl.semaphore_signal(barrier, inc=1, device_id={"section": prev_s, "grp": k}, device_id_type=MESH)
    for device in (dev_a, dev_b, dev_a2, dev_b2, dev_sib):
        pl.semaphore_signal(barrier, inc=1, device_id=device, device_id_type=MESH)

    own_cols = pl.ds(pl.multiple_of(c * HALF, 128), HALF)
    other_cols = pl.ds(pl.multiple_of((1 - c) * HALF, 128), HALF)
    pairs = [
        (scale_hbm, scale_ref), (lat_hbm, lat_ref), (rope_hbm, rope_ref), (dest_hbm, dest),
        (query_hbm, q_in), (reply_hbm, reply_ref), (ctx_len_hbm, ctx_len),
        (uv_hbm, wuv), (out_hbm.at[:, own_cols], wout.at[c]), (vocab_hbm, wvoc),
        (target_hbm, target_ref), (reply_len_hbm, reply_len),
    ]
    local = [pltpu.make_async_copy(a, b, local_sem.at[i]) for i, (a, b) in enumerate(pairs)]
    for copy in local:
        copy.start()

    row = lax.broadcasted_iota(jnp.int32, (64, 64), 0)
    col = lax.broadcasted_iota(jnp.int32, (64, 64), 1)
    place = 2 * ((row // 32) * 16 + row % 16) + (row // 16) % 2
    perm = (col == place).astype(BF16)
    for copy in local[:4]:
        copy.wait()
    scales = jnp.concatenate([scale_ref[j].astype(F32) for j in range(REQ)] + [jnp.zeros((4, 64), F32)], axis=0)
    scales = jnp.concatenate([scales, jnp.zeros((16, 64), F32)], axis=1)
    scales = jnp.transpose(jnp.concatenate([scales] * 8, axis=0))
    for j in range(REQ):
        parts = [
            (lat_ref[j, :, b * 128 : (b + 1) * 128].astype(F32) * scales[0:64, j * 4 + b : j * 4 + b + 1]).astype(BF16)
            for b in range(4)
        ]
        moved = nn_dot(perm, jnp.concatenate(parts, axis=1)).astype(BF16)
        for h in range(2):
            xsrc_a[j, h, :, 0:KVR] = moved[h * 32 : h * 32 + 16]
            xsrc_a[j, h, :, KVR:WIDE_A] = rope_ref[j, h * 16 : (h + 1) * 16, :]
            xsrc_b[j, h] = moved[h * 32 + 16 : h * 32 + 32]

    own_dest = [dest[(s * NG + g) * REQ + j] for j in range(REQ)]
    for h in range(CHUNKS):
        for k in range(NG):
            first = jnp.where(own_dest[0] == k, 0, jnp.where(own_dest[1] == k, 1, 2))
            last = jnp.where(own_dest[2] == k, 2, jnp.where(own_dest[1] == k, 1, 0))
            sbuf[h % 2][h // 2, k, 0] = xsrc[h % 2][first, h // 2]
            sbuf[h % 2][h // 2, k, 1] = xsrc[h % 2][last, h // 2]

    pl.semaphore_wait(barrier, NG + 5)

    def route(h, j):
        k = lax.rem(g + j, NG)
        return pltpu.make_async_remote_copy(
            src_ref=sbuf[h % 2].at[h // 2, k], dst_ref=rbuf[h].at[pl.ds(2 * g, 2)],
            send_sem=route_send.at[h, j], recv_sem=route_recv.at[h, g],
            device_id={"section": next_s, "grp": k}, device_id_type=MESH,
        )

    def route_arrived(h, k):
        return pltpu.make_async_remote_copy(
            src_ref=sbuf[h % 2].at[h // 2, k], dst_ref=rbuf[h].at[pl.ds(2 * k, 2)],
            send_sem=route_send.at[h, k], recv_sem=route_recv.at[h, k],
            device_id={"section": next_s, "grp": k}, device_id_type=MESH,
        )

    def route_start(h):
        for k in range(NG):
            route(h, k).start()

    def route_left(h):
        for k in range(NG):
            route(h, k).wait_send()

    route_start(0)
    w_copy = pltpu.make_async_remote_copy(
        src_ref=out_hbm.at[:, other_cols], dst_ref=wout.at[c],
        send_sem=w_send, recv_sem=w_recv, device_id=dev_sib, device_id_type=MESH,
    )
    w_arrive = pltpu.make_async_remote_copy(
        src_ref=out_hbm.at[:, other_cols], dst_ref=wout.at[1 - c],
        send_sem=w_send, recv_sem=w_recv, device_id=dev_sib, device_id_type=MESH,
    )

    def drain_route():
        route_left(CHUNKS - 1)
        w_copy.wait_send()

    picks = [jnp.int32(0)] * REQ
    count = jnp.int32(0)
    for h in range(NG):
        seen = jnp.int32(0)
        for j in range(REQ):
            hit = dest[(prev_s * NG + h) * REQ + j] == g
            for k in range(REQ):
                picks[k] = jnp.where(jnp.logical_and(hit, count == k), h * 2 + seen, picks[k])
            one = jnp.where(hit, 1, 0)
            seen = seen + one
            count = count + one
    picks = [jnp.minimum(pick, 2 * NG - 1) for pick in picks]

    for copy in local[4:7]:
        copy.wait()
    a_row = (lax.broadcasted_iota(jnp.int32, (QROWS, 32), 0) % 32) // STEPS
    t_row = lax.broadcasted_iota(jnp.int32, (QROWS, 32), 0) % STEPS
    a_col = lax.broadcasted_iota(jnp.int32, (QROWS, 32), 1) % CAND
    u_col = lax.broadcasted_iota(jnp.int32, (QROWS, 32), 1) // CAND
    reply_seen = jnp.logical_and(a_row == a_col, u_col <= t_row)

    def prepare(k, carry):
        slab = q_in[k].astype(F32)
        for h in range(HEADS):
            latent, low, high = unpack_key(slab, h)
            qn[k, h * 32 : (h + 1) * 32, :] = latent.astype(BF16)
            qr[k, h * 32 : (h + 1) * 32, :] = low.astype(BF16)
            qr[k, QROWS + h * 32 : QROWS + (h + 1) * 32, :] = high.astype(BF16)
        keys = reply_ref[k].astype(F32)
        pieces = [unpack_key(keys, u) for u in range(STEPS)]
        rkn[...] = jnp.concatenate([piece[0] for piece in pieces], axis=0).astype(BF16)
        rkr[...] = jnp.concatenate([piece[1] for piece in pieces], axis=0).astype(BF16)
        scores = nt_dot(qn[k], rkn[...]) + nt_dot(qr[k, 0:QROWS], rkr[...])
        scores = jnp.where(reply_seen, scores * softmax_scale, -jnp.inf)
        top = jnp.max(scores, axis=1, keepdims=True)
        weight = jnp.exp(scores - top)
        m_s[k] = top
        l_s[k] = jnp.sum(weight, axis=1, keepdims=True)
        acc_s[k] = nn_dot(weight.astype(BF16), rkn[...])
        return carry

    lax.fori_loop(0, REQ, prepare, 0)

    def ctx_copy(h, slot, way, device):
        block = ctx[h % 2].at[h // 2, slot]
        return pltpu.make_async_remote_copy(
            src_ref=block, dst_ref=block, send_sem=ctx_send.at[h, slot, way], recv_sem=ctx_recv.at[h, slot],
            device_id=device, device_id_type=MESH,
        )

    ctx_ways = (dev_a, dev_b, dev_sib)

    def open_chunk(h):
        for k in range(NG):
            route_arrived(h, k).wait_recv()
        for k in range(REQ):
            ctx[h % 2][h // 2, t, k] = rbuf[h][picks[k]]
        for way in range(3):
            ctx_copy(h, t, way, ctx_ways[way]).start()

    def share(h, slot, *onward):
        ctx_copy(h, slot, 0, dev_a).wait_recv()
        for way in onward:
            ctx_copy(h, slot, way, ctx_ways[way]).start()
        ctx_copy(h, slot, 2, dev_sib).start()

    def hop(h, i):
        share(h, ring(-i) * 2 + c, *((0,) if i < HOP_A else ()))
        if i <= HOP_B:
            share(h, ring(i) * 2 + c, *((1,) if i < HOP_B else ()))

    n_col = lax.broadcasted_iota(jnp.int32, (QROWS, 256), 1)
    n_pos = (n_col // 16) * 64 + 2 * (n_col % 16)

    def attend(h):
        latent, scores = [], []
        for k in range(REQ):
            if h % 2 == 0:
                latent.append(ctx_a[h // 2, :, k, :, 0:KVR].reshape(256, KVR))
            else:
                latent.append(ctx_b[h // 2, :, k].reshape(256, KVR))
            rope = ctx_a[h // 2, :, k, :, KVR:WIDE_A].reshape(256, 128)
            rope_query = qr[k, (h % 2) * QROWS : (h % 2 + 1) * QROWS]
            one = (nt_dot(qn[k], latent[k]) + nt_dot(rope_query, rope)) * softmax_scale
            scores.append(jnp.where(n_pos + (h // 2) * 32 + h % 2 < ctx_len[k], one, -jnp.inf))
        old = [m_s[k] for k in range(REQ)]
        top = [jnp.maximum(old[k], jnp.max(scores[k], axis=1, keepdims=True)) for k in range(REQ)]
        weight = [jnp.exp(scores[k] - top[k]) for k in range(REQ)]
        fade = [jnp.exp(old[k] - top[k]) for k in range(REQ)]
        value = [nn_dot(weight[k].astype(BF16), latent[k]) for k in range(REQ)]
        total = [l_s[k] * fade[k] + jnp.sum(weight[k], axis=1, keepdims=True) for k in range(REQ)]
        for k in range(REQ):
            m_s[k] = top[k]
            l_s[k] = total[k]
            acc_s[k] = acc_s[k] * fade[k] + value[k]

    def close_chunk(h):
        def one(zz, carry):
            ctx_copy(h, zz * 2 + 1 - c, 2, dev_sib).wait_recv()
            return carry

        lax.fori_loop(0, NZ, one, 0)

    for h, i in SCHEDULE:
        if i == ROUTE:
            route_left(h - 1)
            route_start(h)
            if h == CHUNKS - 1:
                w_copy.start()
        elif i == USE:
            close_chunk(h)
            attend(h)
        elif i == 0:
            open_chunk(h)
        else:
            hop(h, i)
    for k in range(REQ):
        rows = (acc_s[k] / l_s[k]).astype(BF16)
        for h in range(HEADS):
            att[h, k * 32 : (k + 1) * 32, :] = rows[h * 32 : (h + 1) * 32]

    def drain_ctx():
        for h in range(CHUNKS):
            for i in range(HOP_A):
                ctx_copy(h, ring(-i) * 2 + c, 0, dev_a).wait_send()
            for i in range(HOP_B):
                ctx_copy(h, ring(i) * 2 + c, 1, dev_b).wait_send()
            for zz in range(NZ):
                ctx_copy(h, zz * 2 + c, 2, dev_sib).wait_send()

    local[7].wait()
    for h in range(HEADS):
        hvbuf[c, :, h * 128 : (h + 1) * 128] = nn_dot(att[h], wuv[:, h * 128 : (h + 1) * 128]).astype(BF16)
    hv_copy = pltpu.make_async_remote_copy(
        src_ref=hvbuf.at[c], dst_ref=hvbuf.at[c], send_sem=hv_send, recv_sem=hv_recv,
        device_id=dev_sib, device_id_type=MESH,
    )
    hv_arrive = pltpu.make_async_remote_copy(
        src_ref=hvbuf.at[1 - c], dst_ref=hvbuf.at[1 - c], send_sem=hv_send, recv_sem=hv_recv,
        device_id=dev_sib, device_id_type=MESH,
    )
    hv_copy.start()
    local[8].wait()
    w_arrive.wait_recv()
    hv_arrive.wait_recv()

    def block_rows(zb):
        return pl.ds(pl.multiple_of((zb // 4) * BR, 16), BR)

    def partials(index, zb):
        cols = pl.ds(pl.multiple_of((zb % 4) * BC, 128), BC)
        both = nn_dot(hvbuf[0], wout[0, :, cols]) + nn_dot(hvbuf[1], wout[1, :, cols])
        part[index, 0] = both[0:BR]
        part[index, 1] = both[BR : 2 * BR]

    targets_of = (dev_a2, dev_a, dev_b, dev_a, dev_b, dev_a2, dev_b2)

    def push(i):
        return pltpu.make_async_remote_copy(
            src_ref=snd.at[i], dst_ref=rcv.at[i], send_sem=r_send.at[i], recv_sem=r_recv.at[i],
            device_id=targets_of[i], device_id_type=MESH,
        )

    def send(i, value):
        snd[i] = value.astype(BF16)
        push(i).start()

    def received(i):
        push(i).wait_recv()
        return rcv[i].astype(F32)

    far, side, back = ring(4), ring(3), ring(-3)
    near_a, near_b, mid_a, mid_b = ring(1), ring(-1), ring(2), ring(-2)
    partials(0, far)
    send(0, part[0, far // 4])
    partials(1, side)
    send(1, part[1, side // 4])
    partials(2, back)
    send(2, part[2, back // 4])
    partials(3, mid_a)
    for i in range(3):
        push(i).wait_send()
    send(3, part[2, near_a // 4])
    send(4, part[1, near_b // 4])
    send(5, part[3, mid_a // 4] + received(0) + received(1))
    send(6, part[3, mid_b // 4] + received(2))
    own = part[0, z // 4] + received(3) + received(4)
    own = own + received(6)
    own = own + received(5)

    def drain_reduce():
        hv_copy.wait_send()
        for i in range(3, 7):
            push(i).wait_send()

    ways = (dev_a, dev_a2, dev_b, dev_b2, dev_sib)

    def hid_copy(zb, way):
        return pltpu.make_async_remote_copy(
            src_ref=hid.at[c, zb], dst_ref=hid.at[c, zb], send_sem=h_send.at[zb, way],
            recv_sem=h_recv.at[c, zb], device_id=ways[way], device_id_type=MESH,
        )

    def hid_sibling(zb):
        return pltpu.make_async_remote_copy(
            src_ref=hid.at[1 - c, zb], dst_ref=hid.at[1 - c, zb], send_sem=h_send.at[zb, 4],
            recv_sem=h_recv.at[1 - c, zb], device_id=dev_sib, device_id_type=MESH,
        )

    lg[...] = jnp.zeros_like(lg)
    ss[...] = jnp.zeros_like(ss)

    def use(core, *blocks):
        products, squares = [], []
        for zb in blocks:
            x = hid[core, zb]
            depth = pl.ds(pl.multiple_of(core * HALF + (zb % 4) * BC, 128), BC)
            products.append(nn_dot(x, wvoc[depth, :]))
            wide = x.astype(F32)
            square = wide * wide
            total = square[:, 0:128]
            for j in range(1, BC // 128):
                total = total + square[:, j * 128 : (j + 1) * 128]
            squares.append(total)
        for zb, product, square in zip(blocks, products, squares):
            rows = block_rows(zb)
            lg[rows, :] += product
            ss[rows, :] += square

    hid[c, z] = own.astype(BF16)
    for way in (1, 3, 4):
        hid_copy(z, way).start()
    hid_copy(z, 1).wait_send()
    hid_copy(z, 3).wait_send()
    hid_copy(z, 0).start()
    hid_copy(z, 2).start()
    local[9].wait()
    use(c, z)

    def take(zb, onward):
        hid_copy(zb, 0).wait_recv()
        for way in onward:
            hid_copy(zb, way).start()
        hid_copy(zb, 4).start()

    def use_sibling(zb):
        hid_sibling(zb).wait_recv()
        use(1 - c, zb)

    use_sibling(z)
    take(ring(-2), (1, 0))
    take(ring(2), (2,))
    use(c, ring(-2))
    use(c, ring(2))
    take(ring(-1), ())
    take(ring(1), ())
    use(c, ring(-1))
    use(c, ring(1))
    for step in (2, -2, 1, -1):
        use_sibling(ring(step))
    take(ring(-3), ())
    take(ring(3), ())
    take(ring(4), ())
    use(c, ring(-3), ring(3), ring(4))
    for step in (3, -3, 4):
        hid_sibling(ring(step)).wait_recv()
    use(1 - c, ring(3), ring(-3), ring(4))

    def drain_hidden():
        hid_copy(z, 0).wait_send()
        hid_copy(z, 2).wait_send()
        hid_copy(ring(-2), 0).wait_send()
        hid_copy(ring(-2), 1).wait_send()
        hid_copy(ring(2), 2).wait_send()
        for zz in range(NZ):
            hid_copy(zz, 4).wait_send()

    local[10].wait()
    lane = lax.broadcasted_iota(jnp.int32, (ROWS, 128), 1)
    wide_targets = jnp.concatenate(
        [target_ref[...].astype(F32), jnp.zeros((REQ, 96), F32)], axis=1
    )
    wide_targets = jnp.concatenate([wide_targets, jnp.zeros((8 - REQ, 128), F32)], axis=0)
    turned = jnp.transpose(jnp.concatenate([wide_targets] * 16, axis=0))
    target_col = jnp.concatenate([turned[0:32, k : k + 1] for k in range(REQ)], axis=0).astype(jnp.int32)
    factor = lax.rsqrt(jnp.sum(ss[...], axis=1, keepdims=True) * (1.0 / D) + norm_epsilon)
    logits = lg[...] * factor
    top = jnp.max(logits, axis=1, keepdims=True)
    total = jnp.sum(jnp.exp(logits - top), axis=1, keepdims=True)
    hit = lax.broadcasted_iota(jnp.int32, (ROWS, VOCAB_LOCAL), 1) == target_col - t * VOCAB_LOCAL
    aimed = jnp.sum(jnp.where(hit, logits, 0.0), axis=1, keepdims=True)
    table = jnp.where(lane == 0, top, jnp.where(lane == 1, total, jnp.where(lane == 2, aimed, 0.0)))
    table = jnp.concatenate([table, jnp.zeros((128 - ROWS, 128), F32)], axis=0)
    stat[t] = jnp.transpose(table)[0:8, :]

    def stat_copy(d):
        return pltpu.make_async_remote_copy(
            src_ref=stat.at[t], dst_ref=stat.at[t], send_sem=st_send.at[d], recv_sem=st_recv.at[t],
            device_id={"tp": lax.rem(t + d, NT)}, device_id_type=MESH,
        )

    def stat_arrive(d):
        peer = lax.rem(t + d, NT)
        return pltpu.make_async_remote_copy(
            src_ref=stat.at[peer], dst_ref=stat.at[peer], send_sem=st_send.at[d], recv_sem=st_recv.at[peer],
            device_id={"tp": peer}, device_id_type=MESH,
        )

    for d in range(1, NT):
        stat_copy(d).start()

    local[11].wait()
    lane1 = lax.broadcasted_iota(jnp.int32, (1, 128), 1)
    lengths = jnp.concatenate([reply_len[...].astype(F32), jnp.zeros((REQ, 120), F32)], axis=1)
    lengths = jnp.concatenate([lengths, jnp.zeros((8 - REQ, 128), F32)], axis=0)
    sub8 = lax.broadcasted_iota(jnp.int32, (8, 128), 0)
    lane8 = lax.broadcasted_iota(jnp.int32, (8, 128), 1)
    sub128 = lax.broadcasted_iota(jnp.int32, (128, 128), 0)
    lane128 = lax.broadcasted_iota(jnp.int32, (128, 128), 1)
    to_lanes = ((lane128 % 32) // STEPS == sub128).astype(BF16)
    lengths = jnp.where(lane8 // 32 == sub8, nn_dot(lengths.astype(BF16), to_lanes), 0.0)
    lengths = jnp.sum(lengths, axis=0, keepdims=True)
    lengths = jnp.where(lane1 < ROWS, lengths, 1.0)

    drain_route()
    drain_ctx()
    drain_reduce()
    drain_hidden()
    for d in range(1, NT):
        stat_arrive(d).wait_recv()
    every = [stat[d] for d in range(NT)]
    joint = functools.reduce(jnp.maximum, [one[0:1] for one in every])
    joint_total = functools.reduce(jnp.add, [one[1:2] * jnp.exp(one[0:1] - joint) for one in every])
    joint_aimed = functools.reduce(jnp.add, [one[2:3] for one in every])
    log_prob = joint_aimed - (joint + jnp.log(joint_total))
    inside = jnp.logical_and((lane1 % STEPS).astype(F32) < lengths, lane1 < ROWS)
    value = jnp.where(inside, log_prob, 0.0) / lengths
    spread = jnp.where(lane8 // 32 == sub8, jnp.broadcast_to(value, (8, 128)), 0.0)
    pick = ((sub128 % 32) // STEPS == lane128).astype(F32)
    summed = lax.dot_general(
        spread, pick, (((1,), (0,)), ((), ())), precision=lax.Precision.HIGHEST, preferred_element_type=F32
    )
    score_ref[...] = summed[0:REQ, 0:CAND]
    for d in range(1, NT):
        stat_copy(d).wait_send()


def per_device(
    ctx_latent, ctx_rope, ctx_scale, dest, ctx_len, queries, reply_keys, reply_len, targets, w_uv, w_out, w_vocab
):
    vmem = pl.BlockSpec(memory_space=pltpu.VMEM)
    smem = pltpu.SMEM
    hbm = pl.BlockSpec(memory_space=pltpu.HBM)
    dma = pltpu.SemaphoreType.DMA
    return pl.pallas_call(
        kernel,
        out_shape=jax.ShapeDtypeStruct((REQ, CAND), F32),
        in_specs=[hbm] * 12,
        out_specs=vmem,
        scratch_shapes=[
            smem((48,), jnp.int32),
            smem((REQ,), jnp.int32),
            pltpu.VMEM((REQ, CAND), jnp.int32),
            pltpu.VMEM((REQ, 64, KVR), BF16),
            pltpu.VMEM((REQ, 32, 128), BF16),
            pltpu.VMEM((REQ, 4, 64), BF16),
            pltpu.VMEM((REQ, CAND, STEPS * KEY), BF16),
            pltpu.VMEM((REQ, 32), jnp.int32),
            pltpu.VMEM((REQ, 2, 16, WIDE_A), BF16),
            pltpu.VMEM((REQ, 2, 16, WIDE_B), BF16),
            pltpu.VMEM((2, NG, 2, 16, WIDE_A), BF16),
            pltpu.VMEM((2, NG, 2, 16, WIDE_B), BF16),
            pltpu.VMEM((NG * 2, 16, WIDE_A), BF16),
            pltpu.VMEM((NG * 2, 16, WIDE_B), BF16),
            pltpu.VMEM((NG * 2, 16, WIDE_A), BF16),
            pltpu.VMEM((NG * 2, 16, WIDE_B), BF16),
            pltpu.VMEM((2, NT, REQ, 16, WIDE_A), BF16),
            pltpu.VMEM((2, NT, REQ, 16, WIDE_B), BF16),
            pltpu.VMEM((REQ, 32, HEADS * KEY), BF16),
            pltpu.VMEM((REQ, QROWS, KVR), BF16),
            pltpu.VMEM((REQ, 2 * QROWS, 128), BF16),
            pltpu.VMEM((32, KVR), BF16),
            pltpu.VMEM((32, 128), BF16),
            pltpu.VMEM((REQ, QROWS, 1), F32),
            pltpu.VMEM((REQ, QROWS, 1), F32),
            pltpu.VMEM((REQ, QROWS, KVR), F32),
            pltpu.VMEM((HEADS, ROWS, KVR), BF16),
            pltpu.VMEM((2, ROWS, 512), BF16),
            pltpu.VMEM((KVR, 512), BF16),
            pltpu.VMEM((2, 512, HALF), BF16),
            pltpu.VMEM((D, VOCAB_LOCAL), BF16),
            pltpu.VMEM((4, 2, BR, BC), F32),
            pltpu.VMEM((7, BR, BC), BF16),
            pltpu.VMEM((7, BR, BC), BF16),
            pltpu.VMEM((2, NZ, BR, BC), BF16),
            pltpu.VMEM((ROWS, VOCAB_LOCAL), F32),
            pltpu.VMEM((ROWS, 128), F32),
            pltpu.VMEM((NT, 8, 128), F32),
            dma((12,)),
            dma((CHUNKS, NG)),
            dma((CHUNKS, NG)),
            dma((CHUNKS, NT, 3)),
            dma((CHUNKS, NT)),
            dma, dma, dma, dma,
            dma((7,)), dma((7,)),
            dma((NZ, 5)), dma((2, NZ)),
            dma((NT,)), dma((NT,)),
        ],
        compiler_params=pltpu.CompilerParams(
            collective_id=0, has_side_effects=True, vmem_limit_bytes=62 * 1024 * 1024
        ),
    )(
        dest, ctx_len, reply_len, ctx_latent, ctx_rope, jnp.swapaxes(ctx_scale, 1, 2), reply_keys, targets,
        queries, w_uv, w_out, w_vocab,
    )


def solution(mesh):
    group = ("section", "grp")
    placed = (
        P(group, "tp", None),
        P(group, "tp", None),
        P(group, "tp", None),
        P(),
        P(group),
        P(group, None, "tp"),
        P(group, None, None),
        P(group, None),
        P(group, None),
        P(None, "tp"),
        P("tp", None),
        P(None, "tp"),
    )
    return jax.shard_map(
        per_device, mesh=mesh, in_specs=placed, out_specs=P(group, None), check_vma=False
    )
```
